256 devices in a mesh: shard: 64 (over z, x, core), grp: 4 (over y).
Axes of the slice: x: 4, y: 4, z: 8, core: 2. Of those that a mesh axis runs over, the one named last changes fastest.
Arguments:
- embed: bfloat16 [131072, 768], P(('shard', 'grp')), may hold values from -700 to 700
- cluster: int32 [131072, 1], P(('shard', 'grp')), may hold values from 0 to 63; in each aligned block of 512 rows (0 to 511, 512 to 1023, ...) at most 16 rows name the same one
Outputs:
- nearest_earlier: float32 [131072], P(('shard', 'grp'))
The draws below stay inside these ranges and needn't reach their ends.
Inputs may be any that keep to these rules, and one draw needn't show every extreme that they name: Within the rows of one device, no cluster occurs more than 16 times.
All inputs are finite; a program needn't handle non-finite values.
Results may differ from the reference program's by a relative error of at most 0.0014.
Values may be sent and summed in bfloat16 or wider, within the bound.
A program may use at most 64 MiB of HBM per device.

```python
import math
import jax
import jax.numpy as jnp
import numpy as np
from jax import lax

D = 768
ROWS_DEV = 512
TOTAL = 131072
CLUSTERS = 64
CAP = 16
MAXC = 4096
N_SHARD = 64


def draw_embed(key, part):
    key = jax.random.fold_in(key, 11)
    key_cols, key_rows, key_main = jax.random.split(key, 3)
    columns = jnp.exp(jax.random.uniform(key_cols, (D,), jnp.float32) * math.log(1.5))
    rows_scale = jnp.exp(jax.random.uniform(key_rows, (TOTAL, 1), jnp.float32) * math.log(10.0)) / 3.0
    noise = jnp.clip(jax.random.normal(key_main, (TOTAL, D), jnp.float32), -6.0, 6.0)
    values = noise * columns[None, :] * rows_scale
    return values.astype(jnp.bfloat16)


def routed_block(rng, own, number, rows, amount, top, limit, slope):
    sequence = jax.random.permutation(rng, amount)
    packed, usual = load_shares(amount, rows * top, limit, slope, True), load_shares(amount, rows * top, limit, slope, False)
    places = jnp.arange(amount)

    def named(lengths, offset_by):
        used = int((lengths > 0).sum())
        fixed = max(1, used // 4)
        passed = fixed + (places - fixed + offset_by * (used - fixed)) % max(1, amount - fixed)
        return jnp.zeros((amount,), jnp.int32).at[sequence[jnp.where(places < fixed, places, passed)]].set(jnp.asarray(lengths, jnp.int32))

    lengths = jnp.where(number % 4 == 0, named(packed, number // 4), named(usual, number - number // 4 - 1))
    mixed = jax.random.permutation(jax.random.fold_in(own, 3), amount)
    donor, receiver = mixed[0:amount // 2 * 2:2], mixed[1:amount // 2 * 2:2]
    slack = jnp.minimum(lengths[donor] - 1, limit - lengths[receiver]) // 2
    slack = jnp.where((donor == sequence[0]) | (receiver == sequence[0]) | (lengths[receiver] == 0), 0, jnp.maximum(slack, 0))
    passed = jax.random.randint(jax.random.fold_in(own, 4), (amount // 2,), 0, 1 << 20) % (slack + 1)
    lengths = lengths.at[donor].add(-passed).at[receiver].add(passed)
    items = jnp.searchsorted(jnp.cumsum(lengths), jnp.arange(rows * top), side="right").astype(jnp.int32)
    grid = items.reshape(top, rows).T
    grid = grid[jax.random.permutation(jax.random.fold_in(own, 1), rows)]
    offset_by = jax.random.randint(jax.random.fold_in(own, 2), (rows, 1), 0, top)
    return jnp.take_along_axis(grid, (jnp.arange(top)[None, :] + offset_by) % top, axis=1)


def load_shares(number_of, total, bound, skew, full):
    loads = [(1 << 20) // math.isqrt(grade ** skew) + 1 for grade in range(1, number_of + 1)]
    largest = bound if full else min(bound, max(-(-total // number_of), total * loads[0] // sum(loads)))
    least = 1 if total - largest >= number_of - 1 else 0
    given, spare = [largest] + [least] * (number_of - 1), total - largest - least * (number_of - 1)
    while spare > 0:
        free = [i for i in range(1, number_of) if given[i] < largest] or [i for i in range(1, number_of) if given[i] < bound]
        pool, budget = sum([loads[i] for i in free]), spare
        for i in free:
            addition = min(bound - given[i], max(1, budget * loads[i] // pool), spare)
            given[i] = given[i] + addition
            spare = spare - addition
    return np.array(given)


def setup_inputs(seed: int = 0) -> dict:
    seeds = jax.random.split(jax.random.key(seed), 3)
    embed = draw_embed(jax.random.fold_in(seeds[2], 71), 0)
    cluster_keys = jax.random.split(jax.random.fold_in(seeds[1], 1), TOTAL // ROWS_DEV)
    cluster_turns = jax.random.permutation(jax.random.fold_in(seeds[1], 3), TOTAL // ROWS_DEV)
    cluster = jax.vmap(lambda own, number: routed_block(jax.random.fold_in(seeds[1], 2), own, number, ROWS_DEV, N_SHARD, 1, CAP, 2))(cluster_keys, cluster_turns).reshape((TOTAL, 1))
    return dict(embed=embed, cluster=cluster)


epsilon = 1e-06

def reference(embed, cluster):
    values = embed.astype(jnp.float32)
    mean_sq = lax.optimization_barrier(jnp.mean(values * values, axis=1, keepdims=True))
    unit = (values * lax.rsqrt(mean_sq + epsilon)).astype(jnp.bfloat16)
    cluster_ids = cluster[:, 0].astype(jnp.int32)
    sorted_rows = jnp.argsort(cluster_ids, stable=True).astype(jnp.int32)
    counts = jnp.zeros((CLUSTERS,), jnp.int32).at[cluster_ids].add(1)
    starts = jnp.cumsum(counts) - counts
    sorted_ids = cluster_ids[sorted_rows]
    position = jnp.arange(TOTAL, dtype=jnp.int32) - starts[sorted_ids]
    table = jnp.full((CLUSTERS, MAXC), TOTAL, jnp.int32).at[sorted_ids, position].set(sorted_rows)
    unit_pad = jnp.concatenate([unit, jnp.zeros((1, D), jnp.bfloat16)], axis=0)

    def per_cluster(row_ids):
        members = unit_pad[row_ids].astype(jnp.float32)
        scores = jnp.dot(members, members.T, precision=lax.Precision.HIGHEST) / D
        lower = jnp.arange(MAXC)[None, :] < jnp.arange(MAXC)[:, None]
        live = (row_ids < TOTAL)[None, :]
        return lax.optimization_barrier(jnp.max(jnp.where(lower & live, scores, jnp.float32(-1.0)), axis=1))
    maxima = lax.map(per_cluster, table)
    result = jnp.zeros((TOTAL + 1,), jnp.float32).at[table.reshape(-1)].set(maxima.reshape(-1))
    return result[:TOTAL]
```

```python
import functools

import jax
import jax.numpy as jnp
from jax import lax
from jax.experimental import pallas as pl
from jax.experimental.pallas import tpu as pltpu
from jax.sharding import PartitionSpec as P

EPSILON = 1e-06
CORES = 2
CHIPS_X = 4
CAP = 16
LANES = 128
MARK = 64.0
LOW = -1e30
MESH = pl.DeviceIdType.MESH
F32 = jnp.float32
BF16 = jnp.bfloat16


def iota(shape, dim):
    return lax.broadcasted_iota(jnp.int32, shape, dim)


def kernel(
    nz, nx, ny, cap,
    cluster_ref, embed_ref, out_ref,
    unit, send, own, peer, best, reply, home,
    send_sem, recv_sem, swap_send_sem, swap_recv_sem, reply_send_sem, reply_recv_sem,
):
    rows, width = embed_ref.shape
    chips = nz * nx * ny
    owners = chips // 2
    half_y = ny // 2
    plane_owners = nx * half_y
    plane_rows = nx * ny * cap
    plane_slots = plane_owners * cap
    group = LANES // cap

    shard, y = lax.axis_index("shard"), lax.axis_index("grp")
    core = shard % CORES
    x = (shard // CORES) % nx
    z = shard // (CORES * nx)
    chip = (z * nx + x) * ny + y
    is_owner = (x + y + z) % 2 == 0
    my_cluster = (z * nx + x) * half_y + y // 2

    def device_of(chip_index):
        return ((chip_index // ny) * CORES + core, chip_index % ny)

    def owner_chip(zo, j):
        xo, h = j // half_y, j % half_y
        return (zo * nx + xo) * ny + 2 * h + (xo + zo) % 2

    peer_device = (shard + 1 - 2 * core, y)

    barrier = pltpu.get_barrier_semaphore()

    def greet(i, _):
        pl.semaphore_signal(
            barrier, inc=1, device_id=device_of((chip + 1 + i) % chips), device_id_type=MESH
        )
        return 0

    lax.fori_loop(0, chips - 1, greet, 0)
    pl.semaphore_signal(barrier, inc=1, device_id=peer_device, device_id_type=MESH)

    values = embed_ref[...].astype(F32)
    mean_sq = jnp.sum(values * values, axis=1, keepdims=True) / width
    unit[...] = (values * lax.rsqrt(mean_sq + EPSILON)).astype(BF16)
    cluster = cluster_ref[...]
    named = iota((owners, rows), 0) == cluster
    earlier = jnp.where(iota((rows, rows), 0) < iota((rows, rows), 1), 1.0, 0.0).astype(BF16)
    named_f32 = jnp.where(named, 1.0, 0.0)
    before = jnp.dot(named_f32.astype(BF16), earlier, preferred_element_type=F32)
    rank = jnp.sum(before * named_f32, axis=0, keepdims=True).astype(jnp.int32)
    slot = cluster * cap + rank

    pl.semaphore_wait(barrier, chips)

    offsets = [nz // 2]
    for step in range(nz // 2 - 1, 0, -1):
        offsets += [step, nz - step]
    offsets += [0]

    for offset in offsets:
        zo = (z + nz - offset) % nz
        first = pl.multiple_of(zo * plane_slots, plane_slots)
        chosen = jnp.where(iota((plane_slots, rows), 0) + first == slot, 1.0, 0.0)
        packed = jnp.dot(chosen.astype(BF16), unit[...], preferred_element_type=F32)
        filled = jnp.sum(chosen, axis=1, keepdims=True)
        send[pl.ds(first, plane_slots), :] = jnp.where(filled > 0.5, packed, MARK).astype(BF16)

        def post(j, _, zo=zo, first=first):
            target = owner_chip(zo, j)
            source = send.at[pl.ds(pl.multiple_of(first + j * cap, cap), cap)]
            landing = own.at[pl.ds(pl.multiple_of(chip * cap, cap), cap)]

            @pl.when(target == chip)
            def _():
                pltpu.make_async_copy(source, landing, recv_sem.at[z]).start()

            @pl.when(target != chip)
            def _():
                pltpu.make_async_remote_copy(
                    source, landing, send_sem, recv_sem.at[z],
                    device_id=device_of(target), device_id_type=MESH,
                ).start()

            return 0

        lax.fori_loop(0, plane_owners, post, 0)

    def plane(ref, index):
        return ref.at[pl.ds(pl.multiple_of(index * plane_rows, plane_rows), plane_rows)]

    def fold(keys, queries, query_plane, limit):
        found = keys[...]
        scores = lax.dot_general(
            found, queries[...], (((1,), (1,)), ((), ())), preferred_element_type=F32
        )
        bias = jnp.where(found[:, :LANES].astype(F32) > 32.0, LOW, 0.0)
        scores = scores + jnp.concatenate([bias] * (plane_rows // LANES), axis=1)
        if limit is not None:
            scores = jnp.where(limit, scores, LOW)
        row = pl.ds(query_plane, 1)
        best[row] = jnp.maximum(best[row], jnp.max(scores, axis=0, keepdims=True)[None])

    @pl.when(is_owner)
    def _():
        best[...] = jnp.full(best.shape, -float(width), F32)
        key_index = iota((plane_rows, plane_rows), 0)
        query_index = iota((plane_rows, plane_rows), 1)
        same_core = key_index < query_index
        per_x = ny * cap
        other_core = key_index // per_x < query_index // per_x + core

        def swap(zs):
            return pltpu.make_async_remote_copy(
                plane(own, zs), plane(peer, zs), swap_send_sem.at[zs], swap_recv_sem.at[zs],
                device_id=peer_device, device_id_type=MESH,
            )

        for step, offset in enumerate(offsets):
            zs = (z + offset) % nz
            pltpu.make_async_copy(plane(own, zs), plane(own, zs), recv_sem.at[zs]).wait()
            swap(zs).start()
            swap(zs).wait_recv()
            fold(plane(own, zs), plane(own, zs), zs, same_core)
            fold(plane(peer, zs), plane(own, zs), zs, other_core)

            def pair(t, _, zs=zs):
                zt = (z + offset_of(t)) % nz
                low, high = jnp.minimum(zs, zt), jnp.maximum(zs, zt)
                fold(plane(own, low), plane(own, high), high, None)
                fold(plane(peer, low), plane(own, high), high, None)
                return 0

            def offset_of(t):
                up = (t + 1) // 2
                return nz // 2 - up + (1 - t % 2) * 2 * up

            lax.fori_loop(0, step, pair, 0)

        result = jnp.maximum(best[...] / width, -1.0)
        pieces = plane_rows // LANES
        for piece in range(pieces):
            for zq in range(nz):
                reply[zq * pieces + piece] = result[zq][:, piece * LANES:(piece + 1) * LANES]

        def answer(i, _):
            target = (chip + 1 + i) % chips
            pltpu.make_async_remote_copy(
                reply.at[pl.ds(target // group, 1)], home.at[pl.ds(my_cluster, 1)],
                reply_send_sem, reply_recv_sem,
                device_id=device_of(target), device_id_type=MESH,
            ).start()
            return 0

        lax.fori_loop(0, chips - 1, answer, 0)
        pltpu.make_async_copy(
            reply.at[pl.ds(chip // group, 1)], home.at[pl.ds(my_cluster, 1)], reply_recv_sem
        ).start()

    waited = home.at[pl.ds(0, owners)]
    pltpu.make_async_copy(waited, waited, reply_recv_sem).wait()
    answers = home[...][:owners, 0, :]
    picked = lax.dot_general(
        answers, named_f32, (((0,), (0,)), ((), ())),
        preferred_element_type=F32, precision=lax.Precision.HIGHEST,
    )
    lane = (chip % group) * cap + rank
    out_ref[...] = jnp.sum(
        jnp.where(iota((LANES, rows), 0) == lane, picked, 0.0), axis=0, keepdims=True
    )

    @pl.when(is_owner)
    def _():
        sent = send.at[pl.ds(0, (owners - 1) * cap)]
        pltpu.make_async_copy(sent, sent, send_sem).wait()
        replied = home.at[pl.ds(0, chips - 1)]
        pltpu.make_async_copy(replied, replied, reply_send_sem).wait()
        for zs in range(nz):
            pltpu.make_async_copy(plane(own, zs), plane(own, zs), swap_send_sem.at[zs]).wait()

    @pl.when(jnp.logical_not(is_owner))
    def _():
        pltpu.make_async_copy(send, send, send_sem).wait()


def on_device(nz, nx, ny, cap, embed, cluster):
    rows, width = embed.shape
    chips = nz * nx * ny
    owners = chips // 2
    out = pl.pallas_call(
        functools.partial(kernel, nz, nx, ny, cap),
        out_shape=jax.ShapeDtypeStruct((1, rows), F32),
        in_specs=[pl.BlockSpec(memory_space=pltpu.VMEM)] * 2,
        out_specs=pl.BlockSpec(memory_space=pltpu.VMEM),
        scratch_shapes=[
            pltpu.VMEM((rows, width), BF16),
            pltpu.VMEM((owners * cap, width), BF16),
            pltpu.VMEM((chips * cap, width), BF16),
            pltpu.VMEM((chips * cap, width), BF16),
            pltpu.VMEM((nz, 1, nx * ny * cap), F32),
            pltpu.VMEM((chips * cap // LANES, 1, LANES), F32),
            pltpu.VMEM((chips, 1, LANES), F32),
            pltpu.SemaphoreType.DMA,
            pltpu.SemaphoreType.DMA((nz,)),
            pltpu.SemaphoreType.DMA((nz,)),
            pltpu.SemaphoreType.DMA((nz,)),
            pltpu.SemaphoreType.DMA,
            pltpu.SemaphoreType.DMA,
        ],
        compiler_params=pltpu.CompilerParams(
            collective_id=0, has_side_effects=True, vmem_limit_bytes=40 * 1024 * 1024
        ),
    )(cluster.reshape(1, rows), embed)
    return out.reshape(rows)


def solution(mesh, nx=CHIPS_X, cap=CAP):
    nz = mesh.shape["shard"] // (CORES * nx)
    ny = mesh.shape["grp"]
    return jax.shard_map(
        functools.partial(on_device, nz, nx, ny, cap),
        mesh=mesh,
        in_specs=(P(("shard", "grp"), None), P(("shard", "grp"), None)),
        out_specs=P(("shard", "grp")),
        check_vma=False,
    )
```

```python
import functools

import jax
import jax.numpy as jnp
from jax import lax
from jax.experimental import pallas as pl
from jax.experimental.pallas import tpu as pltpu
from jax.sharding import PartitionSpec as P

EPSILON = 1e-06
CORES = 2
CHIPS_X = 4
CAP = 16
LANES = 128
MARK = 64.0
LOW = -1e30
MESH = pl.DeviceIdType.MESH
F32 = jnp.float32
BF16 = jnp.bfloat16


def iota(shape, dim):
    return lax.broadcasted_iota(jnp.int32, shape, dim)


def ring_messages(nz):
    far = nz // 2
    messages = [(d, h, u) for d in range(1, far) for h in range(1, d + 1) for u in range(2)]
    return messages + [(far, h, None) for h in range(1, far + 1)]


def kernel(
    nz, nx, ny, cap,
    cluster_ref, embed_ref, out_ref,
    embed, unit, send, ring, own, peer, best, reply, relay, home,
    embed_sem, ring_send, ring_recv, plane_send, plane_recv, swap_send, swap_recv,
    reply_send, relay_recv, home_recv,
):
    rows, width = embed.shape
    far = nz // 2
    places = nx * ny
    owners = nz * places // 2
    half_y = ny // 2
    plane_owners = nx * half_y
    half_owners = plane_owners // 2
    block = plane_owners * cap
    half = block // 2
    plane_rows = places * cap
    pieces = plane_rows // LANES
    group = LANES // cap
    number = {m: i for i, m in enumerate(ring_messages(nz))}

    shard, y = lax.axis_index("shard"), lax.axis_index("grp")
    core = lax.rem(shard, CORES)
    x = lax.rem(lax.div(shard, CORES), nx)
    z = lax.div(shard, CORES * nx)
    place = x * ny + y
    is_owner = lax.rem(x + y + z, 2) == 0
    z_at = [lax.rem(z + o, nz) for o in range(nz)]
    x_at = [lax.rem(x + o, nx) for o in range(nx)]
    y_at = [lax.rem(y + o, ny) for o in range(ny)]
    odd = [lax.rem(z, 2), lax.rem(z + 1, 2)]

    def device(zd, xd, yd):
        return ((zd * nx + xd) * CORES + core, yd)

    peer_device = (shard + 1 - 2 * core, y)
    others = [(ox, oy) for ox in range(nx) for oy in range(ny) if (ox, oy) != (0, 0)]

    fetch = pltpu.make_async_copy(embed_ref, embed, embed_sem)
    fetch.start()

    barrier = pltpu.get_barrier_semaphore()
    partners = [device(z_at[o], x, y) for o in range(1, nz)]
    partners += [device(z, x_at[ox], y_at[oy]) for ox, oy in others]
    partners += [peer_device]
    for partner in partners:
        pl.semaphore_signal(barrier, inc=1, device_id=partner, device_id_type=MESH)

    cluster = cluster_ref[...]
    named = jnp.where(iota((owners, rows), 0) == cluster, 1.0, 0.0)
    earlier = jnp.where(iota((rows, rows), 0) < iota((rows, rows), 1), 1.0, 0.0).astype(BF16)
    before = jnp.dot(named.astype(BF16), earlier, preferred_element_type=F32)
    rank = jnp.sum(before * named, axis=0, keepdims=True).astype(jnp.int32)
    slot = cluster * cap + rank
    fetch.wait()
    values = embed[...].astype(F32)
    mean_sq = jnp.sum(values * values, axis=1, keepdims=True) / width
    unit[...] = (values * lax.rsqrt(mean_sq + EPSILON)).astype(BF16)

    def pack(zo):
        first = pl.multiple_of(zo * block, block)
        chosen = jnp.where(iota((block, rows), 0) + first == slot, 1.0, 0.0)
        packed = jnp.dot(chosen.astype(BF16), unit[...], preferred_element_type=F32)
        filled = jnp.sum(chosen, axis=1, keepdims=True)
        send[pl.ds(first, block), :] = jnp.where(filled > 0.5, packed, MARK).astype(BF16)

    def half_of(direction, message):
        return direction if message[2] is None else message[2]

    def own_half(zo, u):
        return send.at[pl.ds(pl.multiple_of(zo * block + u * half, half), half)]

    def pass_on(direction, message, source):
        index = number[message]
        pltpu.make_async_remote_copy(
            source, ring.at[direction, index], ring_send, ring_recv.at[direction, index],
            device_id=device(z_at[1 if direction == 0 else nz - 1], x, y), device_id_type=MESH,
        ).start()

    def arrived(direction, message):
        index = number[message]
        buffer = ring.at[direction, index]
        pltpu.make_async_copy(buffer, buffer, ring_recv.at[direction, index]).wait()
        return buffer

    def spread(source, u, zs):
        landing = own.at[pl.ds(pl.multiple_of((zs * places + place) * cap, cap), cap)]
        for i in range(half_owners):
            j = u * half_owners + i
            xo, h = j // half_y, j % half_y
            yo = 2 * h + odd[xo % 2]
            mine = (x == xo) & (y == yo)
            part = source.at[pl.ds(i * cap, cap)]

            @pl.when(mine)
            def _():
                pltpu.make_async_copy(part, landing, plane_recv.at[zs]).start()

            @pl.when(jnp.logical_not(mine))
            def _():
                pltpu.make_async_remote_copy(
                    part, landing, plane_send, plane_recv.at[zs],
                    device_id=device(z, xo, yo), device_id_type=MESH,
                ).start()

    def plane(ref, index):
        return ref.at[pl.ds(pl.multiple_of(index * plane_rows, plane_rows), plane_rows)]

    def fold(keys, queries, query_plane, limit):
        found = keys[...]
        scores = lax.dot_general(
            found, queries[...], (((1,), (1,)), ((), ())), preferred_element_type=F32
        )
        bias = jnp.where(found[:, :LANES].astype(F32) > 32.0, LOW, 0.0)
        scores = scores + jnp.concatenate([bias] * pieces, axis=1)
        if limit is not None:
            scores = jnp.where(limit, scores, LOW)
        row = pl.ds(query_plane, 1)
        best[row] = jnp.maximum(best[row], jnp.max(scores, axis=0, keepdims=True)[None])

    def plane_of(t):
        return lax.rem(z + nz + (2 * lax.rem(t, 2) - 1) * lax.div(t + 1, 2), nz)

    def swap(zs):
        return pltpu.make_async_remote_copy(
            plane(own, zs), plane(peer, zs), swap_send.at[zs], swap_recv.at[zs],
            device_id=peer_device, device_id_type=MESH,
        )

    def score(first, last):
        @pl.when(is_owner)
        def _():
            def exchange(s, _):
                zs = plane_of(s)
                pltpu.make_async_copy(plane(own, zs), plane(own, zs), plane_recv.at[zs]).wait()
                swap(zs).start()
                return 0

            def take(s, _):
                swap(plane_of(s)).wait_recv()
                return 0

            def against(ref, shift):
                key = iota((plane_rows, plane_rows), 0)
                query = iota((plane_rows, plane_rows), 1)
                if shift is None:
                    limit = key < query
                else:
                    limit = lax.div(key, ny * cap) < lax.div(query, ny * cap) + shift

                def one(s, _):
                    zs = plane_of(s)
                    fold(plane(ref, zs), plane(own, zs), zs, limit)

                    def pair(t, _):
                        zt = plane_of(t)
                        low, high = jnp.minimum(zs, zt), jnp.maximum(zs, zt)
                        fold(plane(ref, low), plane(own, high), high, None)
                        return 0

                    return lax.fori_loop(0, s, pair, 0)

                lax.fori_loop(first, last + 1, one, 0)

            lax.fori_loop(first, last + 1, exchange, 0)
            against(own, None)
            lax.fori_loop(first, last + 1, take, 0)
            against(peer, core)

    both = ((0, 1), (1, -1))
    pl.semaphore_wait(barrier, len(partners))

    for d in range(1, far + 1):
        for direction, sign in both:
            zo = z_at[sign * d % nz]
            if d < far or direction == 0:
                pack(zo)
            for u in range(2) if d < far else (None,):
                message = (d, 1, u)
                pass_on(direction, message, own_half(zo, half_of(direction, message)))
    pack(z)
    for u in range(2):
        spread(own_half(z, u), u, z)
    best[...] = jnp.full(best.shape, -float(width), F32)

    def step(d, h):
        for u in range(2) if d < far else (None,):
            for direction, sign in both:
                buffer = arrived(direction, (d, h, u))
                if h < d:
                    pass_on(direction, (d, h + 1, u), buffer)
                else:
                    spread(buffer, half_of(direction, (d, h, u)), z_at[-sign * d % nz])

    for h in range(1, far + 1):
        for d in range(h, far + 1):
            step(d, h)
        if h < far - 1:
            score(0 if h == 1 else 2 * h - 1, 2 * h)
    if far > 1:
        score(2 * far - 3 if far > 2 else 0, 2 * far - 2)
    score(2 * far - 1 if far > 1 else 0, 2 * far - 1)

    @pl.when(is_owner)
    def _():
        result = jnp.maximum(best[...] / width, -1.0)
        for piece in range(pieces):
            reply[:, piece] = result[:, :, piece * LANES:(piece + 1) * LANES]
        slab = relay.at[:, lax.div(z, 2)]
        for o in range(1, nz):
            pltpu.make_async_remote_copy(
                reply.at[z_at[o]], slab, reply_send, relay_recv,
                device_id=device(z_at[o], x, y), device_id_type=MESH,
            ).start()
        pltpu.make_async_copy(reply.at[z], slab, relay_recv).start()

    pltpu.make_async_copy(relay, relay, relay_recv).wait()
    for ox, oy in others:
        target = x_at[ox] * ny + y_at[oy]
        pltpu.make_async_remote_copy(
            relay.at[lax.div(target, group)], home.at[place], reply_send, home_recv,
            device_id=device(z, x_at[ox], y_at[oy]), device_id_type=MESH,
        ).start()
    pltpu.make_async_copy(relay.at[lax.div(place, group)], home.at[place], home_recv).start()

    order = iota((owners, 1), 0)
    from_place, level = lax.div(order, far), lax.rem(order, far)
    from_x, from_y = lax.div(from_place, ny), lax.rem(from_place, ny)
    from_z = 2 * level + lax.rem(from_x + from_y, 2)
    held = (from_z * nx + from_x) * half_y + lax.div(from_y, 2)
    wanted = jnp.where(held == cluster, 1.0, 0.0)
    lane = lax.rem(place, group) * cap + rank
    pltpu.make_async_copy(home, home, home_recv).wait()
    answers = home[...].reshape(owners, LANES)
    picked = lax.dot_general(
        answers, wanted, (((0,), (0,)), ((), ())),
        preferred_element_type=F32, precision=lax.Precision.HIGHEST,
    )
    out_ref[...] = jnp.sum(
        jnp.where(iota((LANES, rows), 0) == lane, picked, 0.0), axis=0, keepdims=True
    )

    for direction, _ in both:
        sent = ring.at[direction]
        pltpu.make_async_copy(sent, sent, ring_send).wait()
    replied = home.at[pl.ds(0, places - 1)]
    pltpu.make_async_copy(replied, replied, reply_send).wait()

    @pl.when(is_owner)
    def _():
        passed = send.at[pl.ds(0, nz * (plane_owners - 1) * cap)]
        pltpu.make_async_copy(passed, passed, plane_send).wait()
        told = reply.at[pl.ds(0, nz - 1)]
        pltpu.make_async_copy(told, told, reply_send).wait()
        for zs in range(nz):
            pltpu.make_async_copy(plane(own, zs), plane(own, zs), swap_send.at[zs]).wait()

    @pl.when(jnp.logical_not(is_owner))
    def _():
        pltpu.make_async_copy(send, send, plane_send).wait()


def on_device(nz, nx, ny, cap, embed, cluster):
    rows, width = embed.shape
    places = nx * ny
    slots = nz * places * cap
    messages = len(ring_messages(nz))
    pieces = places * cap // LANES
    out = pl.pallas_call(
        functools.partial(kernel, nz, nx, ny, cap),
        out_shape=jax.ShapeDtypeStruct((1, rows), F32),
        in_specs=[
            pl.BlockSpec(memory_space=pltpu.VMEM),
            pl.BlockSpec(memory_space=pltpu.HBM),
        ],
        out_specs=pl.BlockSpec(memory_space=pltpu.VMEM),
        scratch_shapes=[
            pltpu.VMEM((rows, width), BF16),
            pltpu.VMEM((rows, width), BF16),
            pltpu.VMEM((slots // 2, width), BF16),
            pltpu.VMEM((2, messages, places * cap // 4, width), BF16),
            pltpu.VMEM((slots, width), BF16),
            pltpu.VMEM((slots, width), BF16),
            pltpu.VMEM((nz, 1, places * cap), F32),
            pltpu.VMEM((nz, pieces, 1, LANES), F32),
            pltpu.VMEM((pieces, nz // 2, 1, LANES), F32),
            pltpu.VMEM((places, nz // 2, 1, LANES), F32),
            pltpu.SemaphoreType.DMA,
            pltpu.SemaphoreType.DMA,
            pltpu.SemaphoreType.DMA((2, messages)),
            pltpu.SemaphoreType.DMA,
            pltpu.SemaphoreType.DMA((nz,)),
            pltpu.SemaphoreType.DMA((nz,)),
            pltpu.SemaphoreType.DMA((nz,)),
            pltpu.SemaphoreType.DMA,
            pltpu.SemaphoreType.DMA,
            pltpu.SemaphoreType.DMA,
        ],
        compiler_params=pltpu.CompilerParams(
            collective_id=0, has_side_effects=True, vmem_limit_bytes=40 * 1024 * 1024
        ),
    )(cluster.reshape(1, rows), embed)
    return out.reshape(rows)


def solution(mesh, nx=CHIPS_X, cap=CAP):
    nz = mesh.shape["shard"] // (CORES * nx)
    ny = mesh.shape["grp"]
    return jax.shard_map(
        functools.partial(on_device, nz, nx, ny, cap),
        mesh=mesh,
        in_specs=(P(("shard", "grp"), None), P(("shard", "grp"), None)),
        out_specs=P(("shard", "grp")),
        check_vma=False,
    )
```

```python
import functools

import jax
import jax.numpy as jnp
from jax import lax
from jax.experimental import pallas as pl
from jax.experimental.pallas import tpu as pltpu
from jax.sharding import PartitionSpec as P

EPSILON = 1e-06
CORES = 2
CHIPS_X = 4
CAP = 16
LANES = 128
MARK = 64.0
LOW = -1e30
MESH = pl.DeviceIdType.MESH
F32 = jnp.float32
BF16 = jnp.bfloat16


def iota(shape, dim):
    return lax.broadcasted_iota(jnp.int32, shape, dim)


def ring_messages(nz):
    far = nz // 2
    messages = [(d, h, u) for d in range(1, far) for h in range(1, d + 1) for u in range(2)]
    return messages + [(far, h, None) for h in range(1, far + 1)]


def kernel(
    nz, nx, ny, cap,
    cluster_ref, embed_ref, out_ref,
    embed, unit, send, ring, own, peer, best, reply, relay, home,
    embed_sem, ring_send, ring_recv, plane_send, plane_recv, swap_send, swap_recv,
    reply_send, relay_recv, home_recv,
):
    rows, width = embed.shape
    far = nz // 2
    places = nx * ny
    owners = nz * places // 2
    half_y = ny // 2
    plane_owners = nx * half_y
    half_owners = plane_owners // 2
    block = plane_owners * cap
    half = block // 2
    plane_rows = places * cap
    pieces = plane_rows // LANES
    group = LANES // cap
    number = {m: i for i, m in enumerate(ring_messages(nz))}

    shard, y = lax.axis_index("shard"), lax.axis_index("grp")
    core = lax.rem(shard, CORES)
    x = lax.rem(lax.div(shard, CORES), nx)
    z = lax.div(shard, CORES * nx)
    place = x * ny + y
    is_owner = lax.rem(x + y + z, 2) == 0
    z_at = [lax.rem(z + o, nz) for o in range(nz)]
    x_at = [lax.rem(x + o, nx) for o in range(nx)]
    y_at = [lax.rem(y + o, ny) for o in range(ny)]
    odd = [lax.rem(z, 2), lax.rem(z + 1, 2)]

    def device(zd, xd, yd):
        return ((zd * nx + xd) * CORES + core, yd)

    peer_device = (shard + 1 - 2 * core, y)
    others = [(ox, oy) for ox in range(nx) for oy in range(ny) if (ox, oy) != (0, 0)]

    fetch = pltpu.make_async_copy(embed_ref, embed, embed_sem)
    fetch.start()

    barrier = pltpu.get_barrier_semaphore()
    partners = [device(z_at[o], x, y) for o in range(1, nz)]
    partners += [device(z, x_at[ox], y_at[oy]) for ox, oy in others]
    partners += [peer_device]
    for partner in partners:
        pl.semaphore_signal(barrier, inc=1, device_id=partner, device_id_type=MESH)

    cluster = cluster_ref[...]
    named = jnp.where(iota((owners, rows), 0) == cluster, 1.0, 0.0)
    earlier = jnp.where(iota((rows, rows), 0) < iota((rows, rows), 1), 1.0, 0.0).astype(BF16)
    before = jnp.dot(named.astype(BF16), earlier, preferred_element_type=F32)
    rank = jnp.sum(before * named, axis=0, keepdims=True).astype(jnp.int32)
    slot = cluster * cap + rank
    fetch.wait()
    values = embed[...].astype(F32)
    mean_sq = jnp.sum(values * values, axis=1, keepdims=True) / width
    unit[...] = (values * lax.rsqrt(mean_sq + EPSILON)).astype(BF16)

    def pack(zo):
        first = pl.multiple_of(zo * block, block)
        chosen = jnp.where(iota((block, rows), 0) + first == slot, 1.0, 0.0)
        packed = jnp.dot(chosen.astype(BF16), unit[...], preferred_element_type=F32)
        filled = jnp.sum(chosen, axis=1, keepdims=True)
        send[pl.ds(first, block), :] = jnp.where(filled > 0.5, packed, MARK).astype(BF16)

    def half_of(direction, message):
        return direction if message[2] is None else message[2]

    def own_half(zo, u):
        return send.at[pl.ds(pl.multiple_of(zo * block + u * half, half), half)]

    def pass_on(direction, message, source):
        index = number[message]
        pltpu.make_async_remote_copy(
            source, ring.at[direction, index], ring_send, ring_recv.at[direction, index],
            device_id=device(z_at[1 if direction == 0 else nz - 1], x, y), device_id_type=MESH,
        ).start()

    def arrived(direction, message):
        index = number[message]
        buffer = ring.at[direction, index]
        pltpu.make_async_copy(buffer, buffer, ring_recv.at[direction, index]).wait()
        return buffer

    def spread(source, u, zs):
        landing = own.at[pl.ds(pl.multiple_of((zs * places + place) * cap, cap), cap)]
        for i in range(half_owners):
            j = u * half_owners + i
            xo, h = j // half_y, j % half_y
            yo = 2 * h + odd[xo % 2]
            mine = (x == xo) & (y == yo)
            part = source.at[pl.ds(i * cap, cap)]

            @pl.when(mine)
            def _():
                pltpu.make_async_copy(part, landing, plane_recv.at[zs]).start()

            @pl.when(jnp.logical_not(mine))
            def _():
                pltpu.make_async_remote_copy(
                    part, landing, plane_send, plane_recv.at[zs],
                    device_id=device(z, xo, yo), device_id_type=MESH,
                ).start()

    def plane(ref, index):
        return ref.at[pl.ds(pl.multiple_of(index * plane_rows, plane_rows), plane_rows)]

    def fold(keys, queries, query_plane, limit):
        found = keys[...]
        scores = lax.dot_general(
            found, queries[...], (((1,), (1,)), ((), ())), preferred_element_type=F32
        )
        bias = jnp.where(found[:, :LANES].astype(F32) > 32.0, LOW, 0.0)
        scores = scores + jnp.concatenate([bias] * pieces, axis=1)
        if limit is not None:
            scores = jnp.where(limit, scores, LOW)
        top = jnp.max(scores.reshape(plane_rows // 8, 8, plane_rows), axis=0)
        best[query_plane] = jnp.maximum(best[query_plane], top)

    def plane_of(t):
        return z_at[(2 * (t % 2) - 1) * ((t + 1) // 2) % nz]

    def swap(zs):
        return pltpu.make_async_remote_copy(
            plane(own, zs), plane(peer, zs), swap_send.at[zs], swap_recv.at[zs],
            device_id=peer_device, device_id_type=MESH,
        )

    def score(first, last):
        @pl.when(is_owner)
        def _():
            steps = [plane_of(s) for s in range(last + 1)]

            def against(ref, shift):
                key = iota((plane_rows, plane_rows), 0)
                query = iota((plane_rows, plane_rows), 1)
                if shift is None:
                    limit = key < query
                else:
                    limit = lax.div(key, ny * cap) < lax.div(query, ny * cap) + shift
                for s in range(first, last + 1):
                    zs = steps[s]
                    fold(plane(ref, zs), plane(own, zs), zs, limit)
                    for zt in steps[:s]:
                        low, high = jnp.minimum(zs, zt), jnp.maximum(zs, zt)
                        fold(plane(ref, low), plane(own, high), high, None)

            for zs in steps[first:]:
                pltpu.make_async_copy(plane(own, zs), plane(own, zs), plane_recv.at[zs]).wait()
                swap(zs).start()
            against(own, None)
            for zs in steps[first:]:
                swap(zs).wait_recv()
            against(peer, core)

    both = ((0, 1), (1, -1))
    pl.semaphore_wait(barrier, len(partners))

    for d in range(1, far + 1):
        for direction, sign in both:
            zo = z_at[sign * d % nz]
            if d < far or direction == 0:
                pack(zo)
            for u in range(2) if d < far else (None,):
                message = (d, 1, u)
                pass_on(direction, message, own_half(zo, half_of(direction, message)))
    pack(z)
    for u in range(2):
        spread(own_half(z, u), u, z)
    best[...] = jnp.full(best.shape, -float(width), F32)

    def step(d, h):
        for u in range(2) if d < far else (None,):
            for direction, sign in both:
                buffer = arrived(direction, (d, h, u))
                if h < d:
                    pass_on(direction, (d, h + 1, u), buffer)
                else:
                    spread(buffer, half_of(direction, (d, h, u)), z_at[-sign * d % nz])

    for h in range(1, far + 1):
        for d in range(h, far + 1):
            step(d, h)
        if h == far - 2:
            score(0, 2 * h)
    near = 2 * far - 4
    if far > 1:
        score(near + 1 if far > 2 else 0, near + 2)
    score(2 * far - 1 if far > 1 else 0, 2 * far - 1)

    @pl.when(is_owner)
    def _():
        result = jnp.max(best[...], axis=1, keepdims=True)
        result = jnp.maximum(result / width, -1.0)
        for piece in range(pieces):
            reply[:, piece] = result[:, :, piece * LANES:(piece + 1) * LANES]
        slab = relay.at[:, lax.div(z, 2)]
        for o in range(1, nz):
            pltpu.make_async_remote_copy(
                reply.at[z_at[o]], slab, reply_send, relay_recv,
                device_id=device(z_at[o], x, y), device_id_type=MESH,
            ).start()
        pltpu.make_async_copy(reply.at[z], slab, relay_recv).start()

    pltpu.make_async_copy(relay, relay, relay_recv).wait()
    for ox, oy in others:
        target = x_at[ox] * ny + y_at[oy]
        pltpu.make_async_remote_copy(
            relay.at[lax.div(target, group)], home.at[place], reply_send, home_recv,
            device_id=device(z, x_at[ox], y_at[oy]), device_id_type=MESH,
        ).start()
    pltpu.make_async_copy(relay.at[lax.div(place, group)], home.at[place], home_recv).start()

    order = iota((owners, 1), 0)
    from_place, level = lax.div(order, far), lax.rem(order, far)
    from_x, from_y = lax.div(from_place, ny), lax.rem(from_place, ny)
    from_z = 2 * level + lax.rem(from_x + from_y, 2)
    held = (from_z * nx + from_x) * half_y + lax.div(from_y, 2)
    wanted = jnp.where(held == cluster, 1.0, 0.0)
    lane = lax.rem(place, group) * cap + rank
    pltpu.make_async_copy(home, home, home_recv).wait()
    answers = home[...].reshape(owners, LANES)
    picked = lax.dot_general(
        answers, wanted, (((0,), (0,)), ((), ())),
        preferred_element_type=F32, precision=lax.Precision.HIGHEST,
    )
    out_ref[...] = jnp.sum(
        jnp.where(iota((LANES, rows), 0) == lane, picked, 0.0), axis=0, keepdims=True
    )

    for direction, _ in both:
        sent = ring.at[direction]
        pltpu.make_async_copy(sent, sent, ring_send).wait()
    replied = home.at[pl.ds(0, places - 1)]
    pltpu.make_async_copy(replied, replied, reply_send).wait()

    @pl.when(is_owner)
    def _():
        passed = send.at[pl.ds(0, nz * (plane_owners - 1) * cap)]
        pltpu.make_async_copy(passed, passed, plane_send).wait()
        told = reply.at[pl.ds(0, nz - 1)]
        pltpu.make_async_copy(told, told, reply_send).wait()
        for zs in range(nz):
            pltpu.make_async_copy(plane(own, zs), plane(own, zs), swap_send.at[zs]).wait()

    @pl.when(jnp.logical_not(is_owner))
    def _():
        pltpu.make_async_copy(send, send, plane_send).wait()


def on_device(nz, nx, ny, cap, embed, cluster):
    rows, width = embed.shape
    places = nx * ny
    slots = nz * places * cap
    messages = len(ring_messages(nz))
    pieces = places * cap // LANES
    out = pl.pallas_call(
        functools.partial(kernel, nz, nx, ny, cap),
        out_shape=jax.ShapeDtypeStruct((1, rows), F32),
        in_specs=[
            pl.BlockSpec(memory_space=pltpu.VMEM),
            pl.BlockSpec(memory_space=pltpu.HBM),
        ],
        out_specs=pl.BlockSpec(memory_space=pltpu.VMEM),
        scratch_shapes=[
            pltpu.VMEM((rows, width), BF16),
            pltpu.VMEM((rows, width), BF16),
            pltpu.VMEM((slots // 2, width), BF16),
            pltpu.VMEM((2, messages, places * cap // 4, width), BF16),
            pltpu.VMEM((slots, width), BF16),
            pltpu.VMEM((slots, width), BF16),
            pltpu.VMEM((nz, 8, places * cap), F32),
            pltpu.VMEM((nz, pieces, 1, LANES), F32),
            pltpu.VMEM((pieces, nz // 2, 1, LANES), F32),
            pltpu.VMEM((places, nz // 2, 1, LANES), F32),
            pltpu.SemaphoreType.DMA,
            pltpu.SemaphoreType.DMA,
            pltpu.SemaphoreType.DMA((2, messages)),
            pltpu.SemaphoreType.DMA,
            pltpu.SemaphoreType.DMA((nz,)),
            pltpu.SemaphoreType.DMA((nz,)),
            pltpu.SemaphoreType.DMA((nz,)),
            pltpu.SemaphoreType.DMA,
            pltpu.SemaphoreType.DMA,
            pltpu.SemaphoreType.DMA,
        ],
        compiler_params=pltpu.CompilerParams(
            collective_id=0, has_side_effects=True, vmem_limit_bytes=(64 * 1024 - 256) * 1024
        ),
    )(cluster.reshape(1, rows), embed)
    return out.reshape(rows)


def solution(mesh, nx=CHIPS_X, cap=CAP):
    nz = mesh.shape["shard"] // (CORES * nx)
    ny = mesh.shape["grp"]
    return jax.shard_map(
        functools.partial(on_device, nz, nx, ny, cap),
        mesh=mesh,
        in_specs=(P(("shard", "grp"), None), P(("shard", "grp"), None)),
        out_specs=P(("shard", "grp")),
        check_vma=False,
    )
```

```python
import functools

import jax
import jax.numpy as jnp
from jax import lax
from jax.experimental import pallas as pl
from jax.experimental.pallas import tpu as pltpu
from jax.sharding import PartitionSpec as P

EPSILON = 1e-06
CORES = 2
CAP = 16
LANES = 128
MARK = 64.0
LOW = -1e30
MESH = pl.DeviceIdType.MESH
F32 = jnp.float32
BF16 = jnp.bfloat16


def iota(shape, dim):
    return lax.broadcasted_iota(jnp.int32, shape, dim)


def wait_for(ref, semaphore):
    pltpu.make_async_copy(ref, ref, semaphore).wait()


RING_ORDER = {
    2: ((2, 1, None), (1, 1, 0), (2, 2, None), (1, 1, 1)),
    4: (
        (1, 1, 0), (1, 1, 1), (2, 1, 0), (2, 1, 1), (2, 2, 0), (3, 1, 0), (2, 2, 1), (3, 2, 0),
        (4, 1, None), (3, 1, 1), (4, 2, None), (3, 3, 0), (3, 2, 1), (4, 3, None), (3, 3, 1),
        (4, 4, None),
    ),
}
AHEAD = 4
SPREAD_HERE = 5
OWNER_WORK = {
    2: ((4, "meet", 0, 2), (4, "own", 0, 2), (4, "peer", 0, 2)),
    4: (
        (8, "meet", 0, 2), (9, "own", 0, 2), (10, "peer", 0, 2),
        (11, "meet", 3, 4), (12, "own", 3, 4), (14, "peer", 3, 4),
        (16, "meet", 5, 6), (16, "own", 5, 6),
    ),
}


def kernel(
    nz, side, cap,
    cluster_ref, embed_ref, out_ref,
    cluster_rows, embed, unit, send, lined, ring, own, peer, best, reply, relay, home,
    fetch_sem, line_send, line_recv, ring_send, ring_recv, plane_send, plane_recv,
    swap_send, swap_recv, reply_send, relay_recv, home_recv,
):
    rows, width = embed.shape
    far = nz // 2
    places = side * side
    per_line = side // 2
    owners = nz * side * per_line
    block = side * per_line * cap
    plane_rows = places * cap
    pieces = plane_rows // LANES
    group = LANES // cap
    order = RING_ORDER[far]

    shard, y = lax.axis_index("shard"), lax.axis_index("grp")
    core = lax.rem(shard, CORES)
    x = lax.rem(lax.div(shard, CORES), side)
    z = lax.div(shard, CORES * side)
    a, b = x + core * (y - x), y + core * (x - y)
    place = b * side + a
    is_owner = lax.rem(x + y + z, 2) == 0
    z_at = [lax.rem(z + o, nz) for o in range(nz)]
    a_at = [lax.rem(a + o, side) for o in range(side)]
    b_at = [lax.rem(b + o, side) for o in range(side)]

    def device(zd, ad, bd):
        xd, yd = ad + core * (bd - ad), bd + core * (ad - bd)
        return ((zd * side + xd) * CORES + core, yd)

    peer_device = (shard + 1 - 2 * core, y)
    others = [(oa, ob) for oa in range(side) for ob in range(side) if (oa, ob) != (0, 0)]

    fetch_cluster = pltpu.make_async_copy(cluster_ref, cluster_rows, fetch_sem.at[0])
    fetch_embed = pltpu.make_async_copy(embed_ref, embed, fetch_sem.at[1])
    fetch_cluster.start()
    fetch_embed.start()

    barrier = pltpu.get_barrier_semaphore()
    partners = [device(z_at[o], a, b) for o in range(1, nz)]
    partners += [device(z, a_at[oa], b_at[ob]) for oa, ob in others]
    partners += [peer_device]
    for partner in partners:
        pl.semaphore_signal(barrier, inc=1, device_id=partner, device_id_type=MESH)

    fetch_cluster.wait()
    cluster = cluster_rows[...]
    to_z = lax.div(cluster, side * per_line)
    to_x = lax.rem(lax.div(cluster, per_line), side)
    to_y = 2 * lax.rem(cluster, per_line) + lax.rem(to_x + to_z, 2)
    to_a, to_b = to_x + core * (to_y - to_x), to_y + core * (to_x - to_y)
    owner = (to_z * side + to_a) * per_line + lax.div(to_b, 2)
    named = jnp.where(iota((owners, rows), 0) == owner, 1.0, 0.0)
    earlier = jnp.where(iota((rows, rows), 0) < iota((rows, rows), 1), 1.0, 0.0).astype(BF16)
    before = jnp.dot(named.astype(BF16), earlier, preferred_element_type=F32)
    rank = jnp.sum(before * named, axis=0, keepdims=True).astype(jnp.int32)
    slot = owner * cap + rank

    fetch_embed.wait()
    values = embed[...].astype(F32)
    mean_sq = jnp.sum(values * values, axis=1, keepdims=True) / width
    unit[...] = (values * lax.rsqrt(mean_sq + EPSILON)).astype(BF16)

    def pack(zo):
        chosen = jnp.where(iota((block, rows), 0) + zo * block == slot, 1.0, 0.0)
        packed = jnp.dot(chosen.astype(BF16), unit[...], preferred_element_type=F32)
        filled = jnp.sum(chosen, axis=1, keepdims=True)
        packed = jnp.where(filled > 0.5, packed, MARK).astype(BF16)
        send[pl.ds(zo * side, side)] = packed.reshape(side, per_line, cap, width)

    def line_up(zo):
        pack(zo)
        for o in range(1, side):
            pltpu.make_async_remote_copy(
                send.at[zo * side + a_at[o]], lined.at[zo, a], line_send, line_recv.at[zo],
                device_id=device(z, a_at[o], b), device_id_type=MESH,
            ).start()
        pltpu.make_async_copy(
            send.at[zo * side + a], lined.at[zo, a], line_recv.at[zo]
        ).start()

    def pass_on(direction, index):
        d, h, u = order[index]
        if h == 1:
            zo = z_at[d if direction == 0 else nz - d]
            first = per_line * (direction if u is None else u)
            if d == 1:
                source = send.at[pl.ds(zo * side + first, per_line)]
            else:
                source = lined.at[zo, pl.ds(first, per_line)]
        else:
            source = ring.at[direction, order.index((d, h - 1, u))]
        pltpu.make_async_remote_copy(
            source, ring.at[direction, index], ring_send, ring_recv.at[direction, index],
            device_id=device(z_at[1 if direction == 0 else nz - 1], a, b), device_id_type=MESH,
        ).start()

    def spread(source, first, zs):
        landing = own.at[pl.ds((zs * side + b) * side + first, source.shape[0])]
        for g in range(per_line):
            owner_b = 2 * g + lax.rem(a + z, 2)
            part = source.at[:, g]

            @pl.when(b == owner_b)
            def _():
                pltpu.make_async_copy(part, landing, plane_recv.at[zs]).start()

            @pl.when(b != owner_b)
            def _():
                pltpu.make_async_remote_copy(
                    part, landing, plane_send, plane_recv.at[zs],
                    device_id=device(z, a, owner_b), device_id_type=MESH,
                ).start()

    def spread_near(source, first, zs):
        landing = own.at[(zs * side + b) * side + a]
        for i in range(per_line):
            for g in range(per_line):
                owner_a = first + i
                owner_b = 2 * g + lax.rem(owner_a + z, 2)
                mine = (a == owner_a) & (b == owner_b)

                @pl.when(mine)
                def _():
                    pltpu.make_async_copy(source.at[i, g], landing, plane_recv.at[zs]).start()

                @pl.when(jnp.logical_not(mine))
                def _():
                    pltpu.make_async_remote_copy(
                        source.at[i, g], landing, plane_send, plane_recv.at[zs],
                        device_id=device(z, owner_a, owner_b), device_id_type=MESH,
                    ).start()

    def plane(ref, index):
        return ref.at[pl.ds(index * places, places)]

    def fold(keys, queries, query_plane, limit):
        found = keys[...].reshape(plane_rows, width)
        asked = queries[...].reshape(plane_rows, width)
        scores = lax.dot_general(
            found, asked, (((1,), (1,)), ((), ())), preferred_element_type=F32
        )
        bias = jnp.where(found[:, :LANES].astype(F32) > 32.0, LOW, 0.0)
        scores = scores + jnp.concatenate([bias] * pieces, axis=1)
        if limit is not None:
            scores = jnp.where(limit, scores, LOW)
        top = jnp.max(scores.reshape(plane_rows // 8, 8, plane_rows), axis=0)
        best[query_plane] = jnp.maximum(best[query_plane], top)

    def plane_of(t):
        return z_at[(2 * (t % 2) - 1) * ((t + 1) // 2) % nz]

    def file_order(index, from_core):
        at_b, at_a = lax.div(index, side * cap), lax.rem(lax.div(index, cap), side)
        at_x, at_y = at_a + from_core * (at_b - at_a), at_b + from_core * (at_a - at_b)
        return ((at_x * CORES + from_core) * side + at_y) * cap + lax.rem(index, cap)

    def swap(zs):
        return pltpu.make_async_remote_copy(
            plane(own, zs), plane(peer, zs), swap_send.at[zs], swap_recv.at[zs],
            device_id=peer_device, device_id_type=MESH,
        )

    steps = [plane_of(t) for t in range(nz)]

    def against(ref, from_core, first, last):
        key = file_order(iota((plane_rows, 1), 0), from_core)
        query = file_order(iota((1, plane_rows), 1), core)
        limit = key < query
        for s in range(first, last + 1):
            zs = steps[s]
            fold(plane(ref, zs), plane(own, zs), zs, limit)
            for zt in steps[:s]:
                low, high = jnp.minimum(zs, zt), jnp.maximum(zs, zt)
                fold(plane(ref, low), plane(own, high), high, None)

    def work(what, first, last):
        @pl.when(is_owner)
        def _():
            if what == "meet":
                for zs in steps[first:last + 1]:
                    wait_for(plane(own, zs), plane_recv.at[zs])
                    swap(zs).start()
            elif what == "own":
                against(own, core, first, last)
            else:
                for zs in steps[first:last + 1]:
                    wait_for(plane(peer, zs), swap_recv.at[zs])
                against(peer, 1 - core, first, last)

    ready = [0 if h == 1 else order.index((d, h - 1, u)) + 1 for d, h, u in order]
    begins = [max(0, i + 1 - AHEAD, r) for i, r in enumerate(ready)]
    for i in range(1, len(begins)):
        begins[i] = max(begins[i], begins[i - 1])
    waited = set()
    sent_first = [order.index((1, 1, u)) for u in range(2 if far > 2 else 1)]

    def line_ready(offset):
        if offset not in waited:
            waited.add(offset)
            wait_for(lined.at[z_at[offset]], line_recv.at[z_at[offset]])

    def send_after(count):
        for index, (d, h, _) in enumerate(order):
            if begins[index] == count and index not in sent_first:
                for direction in range(2):
                    if h == 1 and d > 1:
                        line_ready(d if direction == 0 else nz - d)
                    pass_on(direction, index)

    pl.semaphore_wait(barrier, len(partners))
    for offset in (1, nz - 1):
        pack(z_at[offset])
        for index in range(2 if far > 2 else 1):
            pass_on(0 if offset == 1 else 1, order.index((1, 1, index)))
    for offset in [sign * d % nz for d in range(2, far) for sign in (1, -1)] + [far, 0]:
        line_up(z_at[offset])
    send_after(0)
    best[...] = jnp.full(best.shape, -float(width), F32)
    for count, message in enumerate(order, 1):
        d, h, u = message
        for direction in range(2):
            buffer = ring.at[direction, count - 1]
            wait_for(buffer, ring_recv.at[direction, count - 1])
            if h == d:
                zs = z_at[nz - d if direction == 0 else d]
                first = per_line * (direction if u is None else u)
                (spread_near if d == 1 else spread)(buffer, first, zs)
        send_after(count)
        if count == min(SPREAD_HERE, len(order)):
            line_ready(0)
            spread(lined.at[z], 0, z)
        for after, what, first, last in OWNER_WORK[far]:
            if after == count:
                work(what, first, last)
    last = nz - 1
    work("meet", last, last)
    if far > 2:
        work("peer", last - 2, last - 1)
    work("own", last, last)
    work("peer", last, last)

    @pl.when(is_owner)
    def _():
        result = jnp.max(best[...], axis=1, keepdims=True)
        result = jnp.maximum(result / width, -1.0)
        for piece in range(pieces):
            reply[:, piece] = result[:, :, piece * LANES:(piece + 1) * LANES]
        slab = relay.at[:, lax.div(z, 2)]
        for o in range(1, nz):
            pltpu.make_async_remote_copy(
                reply.at[z_at[o]], slab, reply_send, relay_recv,
                device_id=device(z_at[o], a, b), device_id_type=MESH,
            ).start()
        pltpu.make_async_copy(reply.at[z], slab, relay_recv).start()

    wait_for(relay, relay_recv)
    for oa, ob in others:
        target = b_at[ob] * side + a_at[oa]
        pltpu.make_async_remote_copy(
            relay.at[lax.div(target, group)], home.at[place], reply_send, home_recv,
            device_id=device(z, a_at[oa], b_at[ob]), device_id_type=MESH,
        ).start()
    pltpu.make_async_copy(relay.at[lax.div(place, group)], home.at[place], home_recv).start()

    entry = iota((owners, 1), 0)
    from_place, level = lax.div(entry, far), lax.rem(entry, far)
    from_b, from_a = lax.div(from_place, side), lax.rem(from_place, side)
    from_z = 2 * level + lax.rem(from_a + from_b, 2)
    held = (from_z * side + from_a) * per_line + lax.div(from_b, 2)
    wanted = jnp.where(held == owner, 1.0, 0.0)
    lane = lax.rem(place, group) * cap + rank
    wait_for(home, home_recv)
    answers = home[...].reshape(owners, LANES)
    picked = lax.dot_general(
        answers, wanted, (((0,), (0,)), ((), ())),
        preferred_element_type=F32, precision=lax.Precision.HIGHEST,
    )
    out_ref[...] = jnp.sum(
        jnp.where(iota((LANES, rows), 0) == lane, picked, 0.0), axis=0, keepdims=True
    )

    lines = send.at[pl.ds(0, (nz - 2) * (side - 1))]
    wait_for(lines, line_send)
    for direction in range(2):
        sent = ring.at[direction]
        wait_for(sent, ring_send)
    replied = home.at[pl.ds(0, places - 1)]
    wait_for(replied, reply_send)

    @pl.when(is_owner)
    def _():
        passed = 2 * (side * per_line - 1) + (nz - 2) * side * (per_line - 1)
        wait_for(own.at[pl.ds(0, passed)], plane_send)
        told = reply.at[pl.ds(0, nz - 1)]
        wait_for(told, reply_send)
        for zs in range(nz):
            wait_for(plane(own, zs), swap_send.at[zs])

    @pl.when(jnp.logical_not(is_owner))
    def _():
        wait_for(own.at[pl.ds(0, nz * side * per_line)], plane_send)


def on_device(nz, side, cap, embed, cluster):
    rows, width = embed.shape
    places = side * side
    per_line = side // 2
    messages = len(RING_ORDER[nz // 2])
    pieces = places * cap // LANES
    out = pl.pallas_call(
        functools.partial(kernel, nz, side, cap),
        out_shape=jax.ShapeDtypeStruct((1, rows), F32),
        in_specs=[pl.BlockSpec(memory_space=pltpu.HBM)] * 2,
        out_specs=pl.BlockSpec(memory_space=pltpu.VMEM),
        scratch_shapes=[
            pltpu.VMEM((1, rows), jnp.int32),
            pltpu.VMEM((rows, width), BF16),
            pltpu.VMEM((rows, width), BF16),
            pltpu.VMEM((nz * side, per_line, cap, width), BF16),
            pltpu.VMEM((nz, side, per_line, cap, width), BF16),
            pltpu.VMEM((2, messages, per_line, per_line, cap, width), BF16),
            pltpu.VMEM((nz * places, cap, width), BF16),
            pltpu.VMEM((nz * places, cap, width), BF16),
            pltpu.VMEM((nz, 8, places * cap), F32),
            pltpu.VMEM((nz, pieces, 1, LANES), F32),
            pltpu.VMEM((pieces, nz // 2, 1, LANES), F32),
            pltpu.VMEM((places, nz // 2, 1, LANES), F32),
            pltpu.SemaphoreType.DMA((2,)),
            pltpu.SemaphoreType.DMA,
            pltpu.SemaphoreType.DMA((nz,)),
            pltpu.SemaphoreType.DMA,
            pltpu.SemaphoreType.DMA((2, messages)),
            pltpu.SemaphoreType.DMA,
            pltpu.SemaphoreType.DMA((nz,)),
            pltpu.SemaphoreType.DMA((nz,)),
            pltpu.SemaphoreType.DMA((nz,)),
            pltpu.SemaphoreType.DMA,
            pltpu.SemaphoreType.DMA,
            pltpu.SemaphoreType.DMA,
        ],
        compiler_params=pltpu.CompilerParams(
            collective_id=0, has_side_effects=True, vmem_limit_bytes=(64 * 1024 - 512) * 1024
        ),
    )(cluster.reshape(1, rows), embed)
    return out.reshape(rows)


def solution(mesh, cap=CAP):
    side = mesh.shape["grp"]
    nz = mesh.shape["shard"] // (CORES * side)
    return jax.shard_map(
        functools.partial(on_device, nz, side, cap),
        mesh=mesh,
        in_specs=(P(("shard", "grp"), None), P(("shard", "grp"), None)),
        out_specs=P(("shard", "grp")),
        check_vma=False,
    )
```

```python
import functools

import jax
import jax.numpy as jnp
from jax import lax
from jax.experimental import pallas as pl
from jax.experimental.pallas import tpu as pltpu
from jax.sharding import PartitionSpec as P

EPSILON = 1e-06
CORES = 2
CAP = 16
LANES = 128
MARK = 64.0
LOW = -1e30
MESH = pl.DeviceIdType.MESH
F32 = jnp.float32
BF16 = jnp.bfloat16


def iota(shape, dim):
    return lax.broadcasted_iota(jnp.int32, shape, dim)


def wait_for(ref, semaphore):
    pltpu.make_async_copy(ref, ref, semaphore).wait()


RING_ORDER = {
    2: ((2, 1, None), (1, 1, 0), (2, 2, None), (1, 1, 1)),
    4: (
        (1, 1, 0), (1, 1, 1), (2, 1, 0), (2, 1, 1), (2, 2, 0), (3, 1, 0), (2, 2, 1), (3, 2, 0),
        (4, 1, None), (3, 1, 1), (4, 2, None), (3, 3, 0), (3, 2, 1), (4, 3, None), (3, 3, 1),
        (4, 4, None),
    ),
}
AHEAD = 4
SPREAD_HERE = 5
OWNER_WORK = {
    2: ((4, "meet", 0, 2), (4, "own", 0, 2), (4, "peer", 0, 2)),
    4: (
        (8, "meet", 0, 2), (9, "own", 0, 2), (10, "peer", 0, 2),
        (11, "meet", 3, 4), (12, "own", 3, 4), (14, "peer", 3, 4),
        (16, "meet", 5, 6), (16, "own", 5, 6),
    ),
}


def kernel(
    nz, side, cap,
    cluster_ref, embed_ref, out_ref,
    cluster_rows, embed, unit, send, lined, ring, own, peer, best, reply, home,
    fetch_sem, line_send, line_recv, ring_send, ring_recv, plane_send, plane_recv,
    swap_send, swap_recv, reply_send, home_recv,
):
    rows, width = embed.shape
    far = nz // 2
    places = side * side
    per_line = side // 2
    owners = nz * side * per_line
    block = side * per_line * cap
    plane_rows = places * cap
    pieces = plane_rows // LANES
    group = LANES // cap
    order = RING_ORDER[far]

    shard, y = lax.axis_index("shard"), lax.axis_index("grp")
    core = lax.rem(shard, CORES)
    x = lax.rem(lax.div(shard, CORES), side)
    z = lax.div(shard, CORES * side)
    a, b = x + core * (y - x), y + core * (x - y)
    place = b * side + a
    is_owner = lax.rem(x + y + z, 2) == 0
    z_at = [lax.rem(z + o, nz) for o in range(nz)]
    a_at = [lax.rem(a + o, side) for o in range(side)]
    b_at = [lax.rem(b + o, side) for o in range(side)]

    def device(zd, ad, bd):
        xd, yd = ad + core * (bd - ad), bd + core * (ad - bd)
        return ((zd * side + xd) * CORES + core, yd)

    peer_device = (shard + 1 - 2 * core, y)
    others = [(oa, ob) for oa in range(side) for ob in range(side) if (oa, ob) != (0, 0)]

    fetch_cluster = pltpu.make_async_copy(cluster_ref, cluster_rows, fetch_sem.at[0])
    fetch_embed = pltpu.make_async_copy(embed_ref, embed, fetch_sem.at[1])
    fetch_cluster.start()
    fetch_embed.start()

    barrier = pltpu.get_barrier_semaphore()
    partners = [device(z_at[o], a, b) for o in (1, nz - 1)]
    partners += [device(z, a_at[oa], b_at[ob]) for oa, ob in others]
    partners += [peer_device]
    for partner in partners:
        pl.semaphore_signal(barrier, inc=1, device_id=partner, device_id_type=MESH)

    fetch_cluster.wait()
    cluster = cluster_rows[...]
    to_z = lax.div(cluster, side * per_line)
    to_x = lax.rem(lax.div(cluster, per_line), side)
    to_y = 2 * lax.rem(cluster, per_line) + lax.rem(to_x + to_z, 2)
    to_a, to_b = to_x + core * (to_y - to_x), to_y + core * (to_x - to_y)
    owner = (to_z * side + to_a) * per_line + lax.div(to_b, 2)
    named = jnp.where(iota((owners, rows), 0) == owner, 1.0, 0.0)
    earlier = jnp.where(iota((rows, rows), 0) < iota((rows, rows), 1), 1.0, 0.0).astype(BF16)
    before = jnp.dot(named.astype(BF16), earlier, preferred_element_type=F32)
    rank = jnp.sum(before * named, axis=0, keepdims=True).astype(jnp.int32)
    slot = owner * cap + rank

    fetch_embed.wait()
    values = embed[...].astype(F32)
    mean_sq = jnp.sum(values * values, axis=1, keepdims=True) / width
    unit[...] = (values * lax.rsqrt(mean_sq + EPSILON)).astype(BF16)

    def pack(zo):
        chosen = jnp.where(iota((block, rows), 0) + zo * block == slot, 1.0, 0.0)
        packed = jnp.dot(chosen.astype(BF16), unit[...], preferred_element_type=F32)
        filled = jnp.sum(chosen, axis=1, keepdims=True)
        packed = jnp.where(filled > 0.5, packed, MARK).astype(BF16)
        send[pl.ds(zo * side, side)] = packed.reshape(side, per_line, cap, width)

    def line_up(zo):
        pack(zo)
        for o in range(1, side):
            pltpu.make_async_remote_copy(
                send.at[zo * side + a_at[o]], lined.at[zo, a], line_send, line_recv.at[zo],
                device_id=device(z, a_at[o], b), device_id_type=MESH,
            ).start()
        pltpu.make_async_copy(
            send.at[zo * side + a], lined.at[zo, a], line_recv.at[zo]
        ).start()

    def pass_on(direction, index):
        d, h, u = order[index]
        if h == 1:
            zo = z_at[d if direction == 0 else nz - d]
            first = per_line * (direction if u is None else u)
            if d == 1:
                source = send.at[pl.ds(zo * side + first, per_line)]
            else:
                source = lined.at[zo, pl.ds(first, per_line)]
        else:
            source = ring.at[direction, order.index((d, h - 1, u))]
        pltpu.make_async_remote_copy(
            source, ring.at[direction, index], ring_send, ring_recv.at[direction, index],
            device_id=device(z_at[1 if direction == 0 else nz - 1], a, b), device_id_type=MESH,
        ).start()

    def spread(source, first, zs):
        landing = own.at[pl.ds((zs * side + b) * side + first, source.shape[0])]
        for g in range(per_line):
            owner_b = 2 * g + lax.rem(a + z, 2)
            part = source.at[:, g]

            @pl.when(b == owner_b)
            def _():
                pltpu.make_async_copy(part, landing, plane_recv.at[zs]).start()

            @pl.when(b != owner_b)
            def _():
                pltpu.make_async_remote_copy(
                    part, landing, plane_send, plane_recv.at[zs],
                    device_id=device(z, a, owner_b), device_id_type=MESH,
                ).start()

    def spread_near(source, first, zs):
        landing = own.at[(zs * side + b) * side + a]
        for i in range(per_line):
            for g in range(per_line):
                owner_a = first + i
                owner_b = 2 * g + lax.rem(owner_a + z, 2)
                mine = (a == owner_a) & (b == owner_b)

                @pl.when(mine)
                def _():
                    pltpu.make_async_copy(source.at[i, g], landing, plane_recv.at[zs]).start()

                @pl.when(jnp.logical_not(mine))
                def _():
                    pltpu.make_async_remote_copy(
                        source.at[i, g], landing, plane_send, plane_recv.at[zs],
                        device_id=device(z, owner_a, owner_b), device_id_type=MESH,
                    ).start()

    def plane(ref, index):
        return ref.at[pl.ds(index * places, places)]

    def fold(keys, queries, query_plane, limit):
        found = keys[...].reshape(plane_rows, width)
        asked = queries[...].reshape(plane_rows, width)
        scores = lax.dot_general(
            found, asked, (((1,), (1,)), ((), ())), preferred_element_type=F32
        )
        bias = jnp.where(found[:, :LANES].astype(F32) > 32.0, LOW, 0.0)
        scores = scores + jnp.concatenate([bias] * pieces, axis=1)
        if limit is not None:
            scores = jnp.where(limit, scores, LOW)
        top = jnp.max(scores.reshape(plane_rows // 8, 8, plane_rows), axis=0)
        best[query_plane] = jnp.maximum(best[query_plane], top)

    def plane_of(t):
        return z_at[(2 * (t % 2) - 1) * ((t + 1) // 2) % nz]

    def file_order(index, from_core):
        at_b, at_a = lax.div(index, side * cap), lax.rem(lax.div(index, cap), side)
        at_x, at_y = at_a + from_core * (at_b - at_a), at_b + from_core * (at_a - at_b)
        return ((at_x * CORES + from_core) * side + at_y) * cap + lax.rem(index, cap)

    def swap(zs):
        return pltpu.make_async_remote_copy(
            plane(own, zs), plane(peer, zs), swap_send.at[zs], swap_recv.at[zs],
            device_id=peer_device, device_id_type=MESH,
        )

    steps = [plane_of(t) for t in range(nz)]

    def against(ref, from_core, first, last):
        key = file_order(iota((plane_rows, 1), 0), from_core)
        query = file_order(iota((1, plane_rows), 1), core)
        limit = key < query
        for s in range(first, last + 1):
            zs = steps[s]
            fold(plane(ref, zs), plane(own, zs), zs, limit)
            for zt in steps[:s]:
                low, high = jnp.minimum(zs, zt), jnp.maximum(zs, zt)
                fold(plane(ref, low), plane(own, high), high, None)

    def work(what, first, last):
        @pl.when(is_owner)
        def _():
            if what == "meet":
                for zs in steps[first:last + 1]:
                    wait_for(plane(own, zs), plane_recv.at[zs])
                    swap(zs).start()
            elif what == "own":
                against(own, core, first, last)
            else:
                for zs in steps[first:last + 1]:
                    wait_for(plane(peer, zs), swap_recv.at[zs])
                against(peer, 1 - core, first, last)

    ready = [0 if h == 1 else order.index((d, h - 1, u)) + 1 for d, h, u in order]
    begins = [max(0, i + 1 - AHEAD, r) for i, r in enumerate(ready)]
    for i in range(1, len(begins)):
        begins[i] = max(begins[i], begins[i - 1])
    waited = set()
    sent_first = [order.index((1, 1, u)) for u in range(2 if far > 2 else 1)]

    def line_ready(offset):
        if offset not in waited:
            waited.add(offset)
            wait_for(lined.at[z_at[offset]], line_recv.at[z_at[offset]])

    def send_after(count):
        for index, (d, h, _) in enumerate(order):
            if begins[index] == count and index not in sent_first:
                for direction in range(2):
                    if h == 1 and d > 1:
                        line_ready(d if direction == 0 else nz - d)
                    pass_on(direction, index)

    pl.semaphore_wait(barrier, len(partners))
    for offset in (1, nz - 1):
        pack(z_at[offset])
        for index in range(2 if far > 2 else 1):
            pass_on(0 if offset == 1 else 1, order.index((1, 1, index)))
    for offset in [sign * d % nz for d in range(2, far) for sign in (1, -1)] + [far, 0]:
        line_up(z_at[offset])
    send_after(0)
    best[...] = jnp.full(best.shape, -float(width), F32)
    for count, message in enumerate(order, 1):
        d, h, u = message
        for direction in range(2):
            buffer = ring.at[direction, count - 1]
            wait_for(buffer, ring_recv.at[direction, count - 1])
            if h == d:
                zs = z_at[nz - d if direction == 0 else d]
                first = per_line * (direction if u is None else u)
                (spread_near if d == 1 else spread)(buffer, first, zs)
        send_after(count)
        if count == min(SPREAD_HERE, len(order)):
            line_ready(0)
            spread(lined.at[z], 0, z)
        for after, what, first, last in OWNER_WORK[far]:
            if after == count:
                work(what, first, last)
    last = nz - 1
    work("meet", last, last)
    if far > 2:
        work("peer", last - 2, last - 1)
    work("own", last, last)
    work("peer", last, last)

    @pl.when(is_owner)
    def _():
        result = jnp.max(best[...], axis=1, keepdims=True)
        result = jnp.maximum(result / width, -1.0)
        for piece in range(pieces):
            reply[:, piece] = result[:, :, piece * LANES:(piece + 1) * LANES]
        landing = home.at[(z * side + a) * per_line + lax.div(b, 2)]
        for oz in sorted(range(nz), key=lambda o: -min(o, nz - o)):
            for oa in range(side):
                for ob in range(side):
                    if (oz, oa, ob) == (0, 0, 0):
                        continue
                    target = b_at[ob] * side + a_at[oa]
                    pltpu.make_async_remote_copy(
                        reply.at[z_at[oz], lax.div(target, group)], landing,
                        reply_send, home_recv,
                        device_id=device(z_at[oz], a_at[oa], b_at[ob]), device_id_type=MESH,
                    ).start()
        pltpu.make_async_copy(reply.at[z, lax.div(place, group)], landing, home_recv).start()

    lane = lax.rem(place, group) * cap + rank
    answered = home.at[pl.ds(0, owners)]
    wait_for(answered, home_recv)
    answers = answered[...].reshape(owners, LANES)
    picked = lax.dot_general(
        answers, named, (((0,), (0,)), ((), ())),
        preferred_element_type=F32, precision=lax.Precision.HIGHEST,
    )
    out_ref[...] = jnp.sum(
        jnp.where(iota((LANES, rows), 0) == lane, picked, 0.0), axis=0, keepdims=True
    )

    lines = send.at[pl.ds(0, (nz - 2) * (side - 1))]
    wait_for(lines, line_send)
    for direction in range(2):
        sent = ring.at[direction]
        wait_for(sent, ring_send)

    @pl.when(is_owner)
    def _():
        passed = 2 * (side * per_line - 1) + (nz - 2) * side * (per_line - 1)
        wait_for(own.at[pl.ds(0, passed)], plane_send)
        wait_for(home.at[pl.ds(0, nz * places - 1)], reply_send)
        for zs in range(nz):
            wait_for(plane(own, zs), swap_send.at[zs])

    @pl.when(jnp.logical_not(is_owner))
    def _():
        wait_for(own.at[pl.ds(0, nz * side * per_line)], plane_send)


def on_device(nz, side, cap, embed, cluster):
    rows, width = embed.shape
    places = side * side
    per_line = side // 2
    messages = len(RING_ORDER[nz // 2])
    pieces = places * cap // LANES
    out = pl.pallas_call(
        functools.partial(kernel, nz, side, cap),
        out_shape=jax.ShapeDtypeStruct((1, rows), F32),
        in_specs=[pl.BlockSpec(memory_space=pltpu.HBM)] * 2,
        out_specs=pl.BlockSpec(memory_space=pltpu.VMEM),
        scratch_shapes=[
            pltpu.VMEM((1, rows), jnp.int32),
            pltpu.VMEM((rows, width), BF16),
            pltpu.VMEM((rows, width), BF16),
            pltpu.VMEM((nz * side, per_line, cap, width), BF16),
            pltpu.VMEM((nz, side, per_line, cap, width), BF16),
            pltpu.VMEM((2, messages, per_line, per_line, cap, width), BF16),
            pltpu.VMEM((nz * places, cap, width), BF16),
            pltpu.VMEM((nz * places, cap, width), BF16),
            pltpu.VMEM((nz, 8, places * cap), F32),
            pltpu.VMEM((nz, pieces, 1, LANES), F32),
            pltpu.VMEM((nz * places, 1, LANES), F32),
            pltpu.SemaphoreType.DMA((2,)),
            pltpu.SemaphoreType.DMA,
            pltpu.SemaphoreType.DMA((nz,)),
            pltpu.SemaphoreType.DMA,
            pltpu.SemaphoreType.DMA((2, messages)),
            pltpu.SemaphoreType.DMA,
            pltpu.SemaphoreType.DMA((nz,)),
            pltpu.SemaphoreType.DMA((nz,)),
            pltpu.SemaphoreType.DMA((nz,)),
            pltpu.SemaphoreType.DMA,
            pltpu.SemaphoreType.DMA,
        ],
        compiler_params=pltpu.CompilerParams(
            collective_id=0, has_side_effects=True, vmem_limit_bytes=40 * 1024 * 1024
        ),
    )(
        pltpu.with_memory_space_constraint(cluster.reshape(1, rows), pltpu.HBM),
        pltpu.with_memory_space_constraint(embed, pltpu.HBM),
    )
    return out.reshape(rows)


def solution(mesh, cap=CAP):
    side = mesh.shape["grp"]
    nz = mesh.shape["shard"] // (CORES * side)
    return jax.shard_map(
        functools.partial(on_device, nz, side, cap),
        mesh=mesh,
        in_specs=(P(("shard", "grp"), None), P(("shard", "grp"), None)),
        out_specs=P(("shard", "grp")),
        check_vma=False,
    )
```

```python
import functools

import jax
import jax.numpy as jnp
from jax import lax
from jax.experimental import pallas as pl
from jax.experimental.pallas import tpu as pltpu
from jax.sharding import PartitionSpec as P

EPSILON = 1e-06
CORES = 2
CAP = 16
LANES = 128
MARK = 64.0
LOW = -1e30
MESH = pl.DeviceIdType.MESH
F32 = jnp.float32
BF16 = jnp.bfloat16


def iota(shape, dim):
    return lax.broadcasted_iota(jnp.int32, shape, dim)


def wait_for(ref, semaphore):
    pltpu.make_async_copy(ref, ref, semaphore).wait()


RING_ORDER = {
    2: ((2, 1, 0, 1), (1, 1, 0, 1), (2, 2, 0, 1), (1, 1, 1, 1)),
    4: (
        (1, 1, 0, 2), (1, 1, 2, 2), (2, 1, 0, 2), (2, 1, 2, 2), (3, 1, 0, 2), (2, 2, 0, 2),
        (2, 2, 2, 2), (3, 1, 2, 2), (3, 2, 0, 2), (4, 1, 0, 1), (4, 1, 1, 1), (3, 2, 2, 2),
        (3, 3, 0, 2), (4, 2, 0, 1), (4, 2, 1, 1), (3, 3, 2, 1), (4, 3, 0, 1), (4, 3, 1, 1),
        (3, 3, 3, 1), (4, 4, 0, 1), (4, 4, 1, 1),
    ),
}
AHEAD = 4
SPREAD_HERE = 5
OWNER_WORK = {
    2: (
        (4, "meet", 0, 2), (4, "own", 0, 2), (4, "peer", 0, 2),
        (4, "meet", 3, 3), (4, "own", 3, 3), (4, "peer", 3, 3),
    ),
    4: (
        (8, "meet", 0, 2), (9, "own", 0, 2), (10, "peer", 0, 2),
        (12, "meet", 3, 4), (13, "own", 3, 4), (15, "peer", 3, 4),
        (21, "meet", 5, 6), (21, "own", 5, 6), (21, "peer", 5, 5), (21, "meet", 7, 7),
        (21, "peer", 6, 6), (21, "own", 7, 7), (21, "peer", 7, 7),
    ),
}


def kernel(
    nz, side, cap,
    cluster_ref, embed_ref, out_ref,
    cluster_rows, embed, unit, send, lined, ring, own, peer, best, reply, home,
    fetch_sem, line_send, line_recv, ring_send, ring_recv, plane_send, plane_recv,
    swap_send, swap_recv, reply_send, home_recv,
):
    rows, width = embed.shape
    far = nz // 2
    places = side * side
    per_line = side // 2
    owners = nz * side * per_line
    block = side * per_line * cap
    plane_rows = places * cap
    pieces = plane_rows // LANES
    group = LANES // cap
    order = RING_ORDER[far]

    shard, y = lax.axis_index("shard"), lax.axis_index("grp")
    core = lax.rem(shard, CORES)
    x = lax.rem(lax.div(shard, CORES), side)
    z = lax.div(shard, CORES * side)
    a, b = x + core * (y - x), y + core * (x - y)
    place = b * side + a
    is_owner = lax.rem(x + y + z, 2) == 0
    z_at = [lax.rem(z + o, nz) for o in range(nz)]
    a_at = [lax.rem(a + o, side) for o in range(side)]
    b_at = [lax.rem(b + o, side) for o in range(side)]

    def device(zd, ad, bd):
        xd, yd = ad + core * (bd - ad), bd + core * (ad - bd)
        return ((zd * side + xd) * CORES + core, yd)

    peer_device = (shard + 1 - 2 * core, y)
    others = [(oa, ob) for oa in range(side) for ob in range(side) if (oa, ob) != (0, 0)]

    fetch_cluster = pltpu.make_async_copy(cluster_ref, cluster_rows, fetch_sem.at[0])
    fetch_embed = pltpu.make_async_copy(embed_ref, embed, fetch_sem.at[1])
    fetch_cluster.start()
    fetch_embed.start()

    barrier = pltpu.get_barrier_semaphore()
    partners = [device(z_at[o], a, b) for o in (1, nz - 1)]
    partners += [device(z, a_at[oa], b_at[ob]) for oa, ob in others]
    partners += [peer_device]
    for partner in partners:
        pl.semaphore_signal(barrier, inc=1, device_id=partner, device_id_type=MESH)

    fetch_cluster.wait()
    cluster = cluster_rows[...]
    to_z = lax.div(cluster, side * per_line)
    to_x = lax.rem(lax.div(cluster, per_line), side)
    to_y = 2 * lax.rem(cluster, per_line) + lax.rem(to_x + to_z, 2)
    to_a, to_b = to_x + core * (to_y - to_x), to_y + core * (to_x - to_y)
    owner = (to_z * side + to_a) * per_line + lax.div(to_b, 2)
    named = jnp.where(iota((owners, rows), 0) == owner, 1.0, 0.0)
    earlier = jnp.where(iota((rows, rows), 0) < iota((rows, rows), 1), 1.0, 0.0).astype(BF16)
    before = jnp.dot(named.astype(BF16), earlier, preferred_element_type=F32)
    rank = jnp.sum(before * named, axis=0, keepdims=True).astype(jnp.int32)
    slot = owner * cap + rank

    fetch_embed.wait()
    values = embed[...].astype(F32)
    mean_sq = jnp.sum(values * values, axis=1, keepdims=True) / width
    unit[...] = (values * lax.rsqrt(mean_sq + EPSILON)).astype(BF16)

    def pack(zo):
        chosen = jnp.where(iota((block, rows), 0) + zo * block == slot, 1.0, 0.0)
        packed = jnp.dot(chosen.astype(BF16), unit[...], preferred_element_type=F32)
        filled = jnp.sum(chosen, axis=1, keepdims=True)
        packed = jnp.where(filled > 0.5, packed, MARK).astype(BF16)
        send[pl.ds(zo * side, side)] = packed.reshape(side, per_line, cap, width)

    def line_up(zo):
        for o in range(1, side):
            pltpu.make_async_remote_copy(
                send.at[zo * side + a_at[o]], lined.at[zo, a], line_send, line_recv.at[zo],
                device_id=device(z, a_at[o], b), device_id_type=MESH,
            ).start()
        pltpu.make_async_copy(
            send.at[zo * side + a], lined.at[zo, a], line_recv.at[zo]
        ).start()

    def first_of(direction, message):
        return message[2] + (direction * per_line if message[0] == far else 0)

    def held_by(direction, index):
        return ring.at[direction, index, pl.ds(0, order[index][3])]

    def before(index):
        d, h, first, count = order[index]
        for i, (e, hop, start, held) in enumerate(order):
            if (e, hop) == (d, h - 1) and start <= first and first + count <= start + held:
                return i, first - start
        return -1, 0

    def pass_on(direction, index):
        d, h, _, count = order[index]
        if h > 1:
            source, start = before(index)
            source = ring.at[direction, source, pl.ds(start, count)]
        else:
            zo = z_at[d if direction == 0 else nz - d]
            first = first_of(direction, order[index])
            if d == 1:
                source = send.at[pl.ds(zo * side + first, count)]
            else:
                source = lined.at[zo, pl.ds(first, count)]
        pltpu.make_async_remote_copy(
            source, held_by(direction, index), ring_send, ring_recv.at[direction, index],
            device_id=device(z_at[1 if direction == 0 else nz - 1], a, b), device_id_type=MESH,
        ).start()

    def spread(source, first, zs):
        landing = own.at[pl.ds((zs * side + b) * side + first, source.shape[0])]
        for g in range(per_line):
            owner_b = 2 * g + lax.rem(a + z, 2)
            part = source.at[:, g]

            @pl.when(b == owner_b)
            def _():
                pltpu.make_async_copy(part, landing, plane_recv.at[zs]).start()

            @pl.when(b != owner_b)
            def _():
                pltpu.make_async_remote_copy(
                    part, landing, plane_send, plane_recv.at[zs],
                    device_id=device(z, a, owner_b), device_id_type=MESH,
                ).start()

    def spread_near(source, first, zs):
        landing = own.at[(zs * side + b) * side + a]
        for i in range(per_line):
            for g in range(per_line):
                owner_a = first + i
                owner_b = 2 * g + lax.rem(owner_a + z, 2)
                mine = (a == owner_a) & (b == owner_b)

                @pl.when(mine)
                def _():
                    pltpu.make_async_copy(source.at[i, g], landing, plane_recv.at[zs]).start()

                @pl.when(jnp.logical_not(mine))
                def _():
                    pltpu.make_async_remote_copy(
                        source.at[i, g], landing, plane_send, plane_recv.at[zs],
                        device_id=device(z, owner_a, owner_b), device_id_type=MESH,
                    ).start()

    def plane(ref, index):
        return ref.at[pl.ds(index * places, places)]

    def fold(keys, queries, query_plane, limit):
        found = keys[...].reshape(plane_rows, width)
        asked = queries[...].reshape(plane_rows, width)
        scores = lax.dot_general(
            found, asked, (((1,), (1,)), ((), ())), preferred_element_type=F32
        )
        bias = jnp.where(found[:, :LANES].astype(F32) > 32.0, LOW, 0.0)
        scores = scores + jnp.concatenate([bias] * pieces, axis=1)
        if limit is not None:
            scores = jnp.where(limit, scores, LOW)
        top = jnp.max(scores.reshape(plane_rows // 8, 8, plane_rows), axis=0)
        best[query_plane] = jnp.maximum(best[query_plane], top)

    def plane_of(t):
        return z_at[(2 * (t % 2) - 1) * ((t + 1) // 2) % nz]

    def file_order(index, from_core):
        at_b, at_a = lax.div(index, side * cap), lax.rem(lax.div(index, cap), side)
        at_x, at_y = at_a + from_core * (at_b - at_a), at_b + from_core * (at_a - at_b)
        return ((at_x * CORES + from_core) * side + at_y) * cap + lax.rem(index, cap)

    def swap(zs):
        return pltpu.make_async_remote_copy(
            plane(own, zs), plane(peer, zs), swap_send.at[zs], swap_recv.at[zs],
            device_id=peer_device, device_id_type=MESH,
        )

    steps = [plane_of(t) for t in range(nz)]

    def against(ref, from_core, first, last):
        key = file_order(iota((plane_rows, 1), 0), from_core)
        query = file_order(iota((1, plane_rows), 1), core)
        limit = key < query
        for s in range(first, last + 1):
            zs = steps[s]
            fold(plane(ref, zs), plane(own, zs), zs, limit)
            for zt in steps[:s]:
                low, high = jnp.minimum(zs, zt), jnp.maximum(zs, zt)
                fold(plane(ref, low), plane(own, high), high, None)

    def work(what, first, last):
        @pl.when(is_owner)
        def _():
            if what == "meet":
                for zs in steps[first:last + 1]:
                    wait_for(plane(own, zs), plane_recv.at[zs])
                    swap(zs).start()
            elif what == "own":
                against(own, core, first, last)
            else:
                for zs in steps[first:last + 1]:
                    wait_for(plane(peer, zs), swap_recv.at[zs])
                against(peer, 1 - core, first, last)

    ready = [before(i)[0] + 1 if h > 1 else min(1, d // 3) for i, (d, h, _, _) in enumerate(order)]
    begins = [max(0, i + 1 - AHEAD, r) for i, r in enumerate(ready)]
    for i in range(1, len(begins)):
        begins[i] = max(begins[i], begins[i - 1])
    waited = set()
    sent_first = [i for i in range(2) if order[i][0] == 1]

    def line_ready(offset):
        if offset not in waited:
            waited.add(offset)
            wait_for(lined.at[z_at[offset]], line_recv.at[z_at[offset]])

    def send_after(count, direction):
        for index, (d, h, _, _) in enumerate(order):
            if begins[index] == count and index not in sent_first:
                if h == 1 and d > 1:
                    line_ready(d if direction == 0 else nz - d)
                pass_on(direction, index)

    pl.semaphore_wait(barrier, len(partners))
    for offset in (1, nz - 1):
        pack(z_at[offset])
        for index in sent_first:
            pass_on(0 if offset == 1 else 1, index)
    for offset in [sign * d % nz for d in range(2, far) for sign in (1, -1)] + [far, 0]:
        pack(z_at[offset])
        line_up(z_at[offset])
    for direction in range(2):
        send_after(0, direction)
    best[...] = jnp.full(best.shape, -float(width), F32)
    for count, message in enumerate(order, 1):
        d, h, _, _ = message
        for direction in range(2):
            buffer = held_by(direction, count - 1)
            wait_for(buffer, ring_recv.at[direction, count - 1])
            send_after(count, direction)
            if h == d:
                zs = z_at[nz - d if direction == 0 else d]
                first = first_of(direction, message)
                (spread_near if d == 1 else spread)(buffer, first, zs)
        if count == min(SPREAD_HERE, len(order)):
            line_ready(0)
            spread(lined.at[z], 0, z)
        for after, what, first, last in OWNER_WORK[far]:
            if after == count:
                work(what, first, last)
    @pl.when(is_owner)
    def _():
        result = jnp.max(best[...], axis=1, keepdims=True)
        result = jnp.maximum(result / width, -1.0)
        for piece in range(pieces):
            reply[:, piece] = result[:, :, piece * LANES:(piece + 1) * LANES]
        landing = home.at[(z * side + a) * per_line + lax.div(b, 2)]
        for oz in sorted(range(nz), key=lambda o: -min(o, nz - o)):
            for oa in range(side):
                for ob in range(side):
                    if (oz, oa, ob) == (0, 0, 0):
                        continue
                    target = b_at[ob] * side + a_at[oa]
                    pltpu.make_async_remote_copy(
                        reply.at[z_at[oz], lax.div(target, group)], landing,
                        reply_send, home_recv,
                        device_id=device(z_at[oz], a_at[oa], b_at[ob]), device_id_type=MESH,
                    ).start()
        pltpu.make_async_copy(reply.at[z, lax.div(place, group)], landing, home_recv).start()

    lane = lax.rem(place, group) * cap + rank
    wanted = jnp.concatenate([named.astype(BF16)] * 3, axis=0)
    answered = home.at[pl.ds(0, owners)]
    wait_for(answered, home_recv)
    left = answered[...].reshape(owners, LANES)
    split = []
    for _ in range(3):
        split.append(left.astype(BF16))
        left = left - split[-1].astype(F32)
    picked = lax.dot_general(
        jnp.concatenate(split, axis=0), wanted, (((0,), (0,)), ((), ())),
        preferred_element_type=F32,
    )
    out_ref[...] = jnp.sum(
        jnp.where(iota((LANES, rows), 0) == lane, picked, 0.0), axis=0, keepdims=True
    )

    lines = send.at[pl.ds(0, (nz - 2) * (side - 1))]
    wait_for(lines, line_send)
    for direction in range(2):
        parts = sum(message[3] for message in order) // per_line
        wait_for(ring.at[direction, pl.ds(0, parts)], ring_send)

    @pl.when(is_owner)
    def _():
        passed = 2 * (side * per_line - 1) + (nz - 2) * side * (per_line - 1)
        wait_for(own.at[pl.ds(0, passed)], plane_send)
        wait_for(home.at[pl.ds(0, nz * places - 1)], reply_send)
        for zs in range(nz):
            wait_for(plane(own, zs), swap_send.at[zs])

    @pl.when(jnp.logical_not(is_owner))
    def _():
        wait_for(own.at[pl.ds(0, nz * side * per_line)], plane_send)


def on_device(nz, side, cap, embed, cluster):
    rows, width = embed.shape
    places = side * side
    per_line = side // 2
    messages = len(RING_ORDER[nz // 2])
    pieces = places * cap // LANES
    out = pl.pallas_call(
        functools.partial(kernel, nz, side, cap),
        out_shape=jax.ShapeDtypeStruct((1, rows), F32),
        in_specs=[pl.BlockSpec(memory_space=pltpu.HBM)] * 2,
        out_specs=pl.BlockSpec(memory_space=pltpu.VMEM),
        scratch_shapes=[
            pltpu.VMEM((1, rows), jnp.int32),
            pltpu.VMEM((rows, width), BF16),
            pltpu.VMEM((rows, width), BF16),
            pltpu.VMEM((nz * side, per_line, cap, width), BF16),
            pltpu.VMEM((nz, side, per_line, cap, width), BF16),
            pltpu.VMEM((2, messages, per_line, per_line, cap, width), BF16),
            pltpu.VMEM((nz * places, cap, width), BF16),
            pltpu.VMEM((nz * places, cap, width), BF16),
            pltpu.VMEM((nz, 8, places * cap), F32),
            pltpu.VMEM((nz, pieces, 1, LANES), F32),
            pltpu.VMEM((nz * places, 1, LANES), F32),
            pltpu.SemaphoreType.DMA((2,)),
            pltpu.SemaphoreType.DMA,
            pltpu.SemaphoreType.DMA((nz,)),
            pltpu.SemaphoreType.DMA,
            pltpu.SemaphoreType.DMA((2, messages)),
            pltpu.SemaphoreType.DMA,
            pltpu.SemaphoreType.DMA((nz,)),
            pltpu.SemaphoreType.DMA((nz,)),
            pltpu.SemaphoreType.DMA((nz,)),
            pltpu.SemaphoreType.DMA,
            pltpu.SemaphoreType.DMA,
        ],
        compiler_params=pltpu.CompilerParams(
            collective_id=0, has_side_effects=True, vmem_limit_bytes=40 * 1024 * 1024
        ),
    )(
        pltpu.with_memory_space_constraint(cluster.reshape(1, rows), pltpu.HBM),
        pltpu.with_memory_space_constraint(embed, pltpu.HBM),
    )
    return out.reshape(rows)


def solution(mesh, cap=CAP):
    side = mesh.shape["grp"]
    nz = mesh.shape["shard"] // (CORES * side)
    return jax.shard_map(
        functools.partial(on_device, nz, side, cap),
        mesh=mesh,
        in_specs=(P(("shard", "grp"), None), P(("shard", "grp"), None)),
        out_specs=P(("shard", "grp")),
        check_vma=False,
    )
```

```python
import functools

import jax
import jax.numpy as jnp
from jax import lax
from jax.experimental import pallas as pl
from jax.experimental.pallas import tpu as pltpu
from jax.sharding import PartitionSpec as P

EPSILON = 1e-06
CORES = 2
CAP = 16
LANES = 128
MARK = 64.0
LOW = -1e30
MESH = pl.DeviceIdType.MESH
F32 = jnp.float32
BF16 = jnp.bfloat16


def iota(shape, dim):
    return lax.broadcasted_iota(jnp.int32, shape, dim)


def wait_for(ref, semaphore):
    pltpu.make_async_copy(ref, ref, semaphore).wait()


RING_ORDER = {
    2: ((2, 1, 0, 1), (1, 1, 0, 1), (2, 2, 0, 1), (1, 1, 1, 1)),
    4: (
        (1, 1, 0, 2), (1, 1, 2, 2), (2, 1, 0, 2), (2, 1, 2, 2), (3, 1, 0, 2), (2, 2, 0, 2),
        (2, 2, 2, 2), (3, 1, 2, 2), (3, 2, 0, 2), (4, 1, 0, 1), (4, 1, 1, 1), (3, 2, 2, 2),
        (3, 3, 0, 2), (4, 2, 0, 1), (4, 2, 1, 1), (3, 3, 2, 1), (4, 3, 0, 1), (4, 3, 1, 1),
        (3, 3, 3, 1), (4, 4, 0, 1), (4, 4, 1, 1),
    ),
}
AHEAD = 4
SPREAD_HERE = 5
OWNER_WORK = {
    2: (
        (4, "meet", 0, 2), (4, "own", 0, 2), (4, "peer", 0, 2),
        (4, "meet", 3, 3), (4, "own", 3, 3), (4, "peer", 3, 3),
    ),
    4: (
        (6, "meet", 0, 2), (7, "own", 0, 2), (8, "peer", 0, 2),
        (9, "meet", 3, 4), (10, "own", 3, 4), (12, "peer", 3, 4),
        (21, "meet", 5, 6), (21, "own", 5, 6), (21, "peer", 5, 5), (21, "meet", 7, 7),
        (21, "peer", 6, 6), (21, "own", 7, 7), (21, "peer", 7, 7),
    ),
}


def kernel(
    nz, side, cap,
    cluster_ref, embed_ref, out_ref,
    cluster_rows, embed, unit, send, lined, ring, own, peer, best, reply, home,
    fetch_sem, line_send, line_recv, ring_send, ring_recv, plane_send, plane_recv,
    swap_send, swap_recv, reply_send, home_recv,
):
    rows, width = embed.shape
    far = nz // 2
    places = side * side
    per_line = side // 2
    owners = nz * side * per_line
    block = side * per_line * cap
    plane_rows = places * cap
    pieces = plane_rows // LANES
    group = LANES // cap
    order = RING_ORDER[far]

    shard, y = lax.axis_index("shard"), lax.axis_index("grp")
    core = lax.rem(shard, CORES)
    x = lax.rem(lax.div(shard, CORES), side)
    z = lax.div(shard, CORES * side)
    a, b = x + core * (y - x), y + core * (x - y)
    place = b * side + a
    is_owner = lax.rem(x + y + z, 2) == 0
    z_at = [lax.rem(z + o, nz) for o in range(nz)]
    a_at = [lax.rem(a + o, side) for o in range(side)]
    b_at = [lax.rem(b + o, side) for o in range(side)]

    def device(zd, ad, bd):
        xd, yd = ad + core * (bd - ad), bd + core * (ad - bd)
        return ((zd * side + xd) * CORES + core, yd)

    peer_device = (shard + 1 - 2 * core, y)
    others = [(oa, ob) for oa in range(side) for ob in range(side) if (oa, ob) != (0, 0)]

    fetch_cluster = pltpu.make_async_copy(cluster_ref, cluster_rows, fetch_sem.at[0])
    fetch_embed = pltpu.make_async_copy(embed_ref, embed, fetch_sem.at[1])
    fetch_cluster.start()
    fetch_embed.start()

    barrier = pltpu.get_barrier_semaphore()
    partners = [device(z_at[o], a, b) for o in (1, nz - 1)]
    partners += [device(z, a_at[oa], b_at[ob]) for oa, ob in others]
    partners += [peer_device]
    for partner in partners:
        pl.semaphore_signal(barrier, inc=1, device_id=partner, device_id_type=MESH)

    fetch_cluster.wait()
    cluster = cluster_rows[...]
    to_z = lax.div(cluster, side * per_line)
    to_x = lax.rem(lax.div(cluster, per_line), side)
    to_y = 2 * lax.rem(cluster, per_line) + lax.rem(to_x + to_z, 2)
    to_a, to_b = to_x + core * (to_y - to_x), to_y + core * (to_x - to_y)
    owner = (to_z * side + to_a) * per_line + lax.div(to_b, 2)
    named = jnp.where(iota((owners, rows), 0) == owner, 1.0, 0.0)
    earlier = jnp.where(iota((rows, rows), 0) < iota((rows, rows), 1), 1.0, 0.0).astype(BF16)
    before = jnp.dot(named.astype(BF16), earlier, preferred_element_type=F32)
    rank = jnp.sum(before * named, axis=0, keepdims=True).astype(jnp.int32)
    slot = owner * cap + rank

    fetch_embed.wait()
    values = embed[...].astype(F32)
    mean_sq = jnp.sum(values * values, axis=1, keepdims=True) / width
    unit[...] = (values * lax.rsqrt(mean_sq + EPSILON)).astype(BF16)

    def pack(zo):
        chosen = jnp.where(iota((block, rows), 0) + zo * block == slot, 1.0, 0.0)
        packed = jnp.dot(chosen.astype(BF16), unit[...], preferred_element_type=F32)
        filled = jnp.sum(chosen, axis=1, keepdims=True)
        packed = jnp.where(filled > 0.5, packed, MARK).astype(BF16)
        send[pl.ds(zo * side, side)] = packed.reshape(side, per_line, cap, width)

    def line_up(zo):
        for o in range(1, side):
            pltpu.make_async_remote_copy(
                send.at[zo * side + a_at[o]], lined.at[zo, a], line_send, line_recv.at[zo],
                device_id=device(z, a_at[o], b), device_id_type=MESH,
            ).start()
        pltpu.make_async_copy(
            send.at[zo * side + a], lined.at[zo, a], line_recv.at[zo]
        ).start()

    def first_of(direction, message):
        return message[2] + (direction * per_line if message[0] == far else 0)

    def held_by(direction, index):
        return ring.at[direction, index, pl.ds(0, order[index][3])]

    def before(index):
        d, h, first, count = order[index]
        for i, (e, hop, start, held) in enumerate(order):
            if (e, hop) == (d, h - 1) and start <= first and first + count <= start + held:
                return i, first - start
        return -1, 0

    def pass_on(direction, index):
        d, h, _, count = order[index]
        if h > 1:
            source, start = before(index)
            source = ring.at[direction, source, pl.ds(start, count)]
        else:
            zo = z_at[d if direction == 0 else nz - d]
            first = first_of(direction, order[index])
            if d == 1:
                source = send.at[pl.ds(zo * side + first, count)]
            else:
                source = lined.at[zo, pl.ds(first, count)]
        pltpu.make_async_remote_copy(
            source, held_by(direction, index), ring_send, ring_recv.at[direction, index],
            device_id=device(z_at[1 if direction == 0 else nz - 1], a, b), device_id_type=MESH,
        ).start()

    def spread(source, first, zs):
        landing = own.at[pl.ds((zs * side + b) * side + first, source.shape[0])]
        for g in range(per_line):
            owner_b = 2 * g + lax.rem(a + z, 2)
            part = source.at[:, g]

            @pl.when(b == owner_b)
            def _():
                pltpu.make_async_copy(part, landing, plane_recv.at[zs]).start()

            @pl.when(b != owner_b)
            def _():
                pltpu.make_async_remote_copy(
                    part, landing, plane_send, plane_recv.at[zs],
                    device_id=device(z, a, owner_b), device_id_type=MESH,
                ).start()

    def spread_near(source, first, zs):
        landing = own.at[(zs * side + b) * side + a]
        for i in range(per_line):
            for g in range(per_line):
                owner_a = first + i
                owner_b = 2 * g + lax.rem(owner_a + z, 2)
                mine = (a == owner_a) & (b == owner_b)

                @pl.when(mine)
                def _():
                    pltpu.make_async_copy(source.at[i, g], landing, plane_recv.at[zs]).start()

                @pl.when(jnp.logical_not(mine))
                def _():
                    pltpu.make_async_remote_copy(
                        source.at[i, g], landing, plane_send, plane_recv.at[zs],
                        device_id=device(z, owner_a, owner_b), device_id_type=MESH,
                    ).start()

    def plane(ref, index):
        return ref.at[pl.ds(index * places, places)]

    def fold(keys, queries, query_plane, limit):
        found = keys[...].reshape(plane_rows, width)
        asked = queries[...].reshape(plane_rows, width)
        scores = lax.dot_general(
            found, asked, (((1,), (1,)), ((), ())), preferred_element_type=F32
        )
        bias = jnp.where(found[:, :LANES].astype(F32) > 32.0, LOW, 0.0)
        scores = scores + jnp.concatenate([bias] * pieces, axis=1)
        if limit is not None:
            scores = jnp.where(limit, scores, LOW)
        top = jnp.max(scores.reshape(plane_rows // 8, 8, plane_rows), axis=0)
        best[query_plane] = jnp.maximum(best[query_plane], top)

    def plane_of(t):
        return z_at[(2 * (t % 2) - 1) * ((t + 1) // 2) % nz]

    def file_order(index, from_core):
        at_b, at_a = lax.div(index, side * cap), lax.rem(lax.div(index, cap), side)
        at_x, at_y = at_a + from_core * (at_b - at_a), at_b + from_core * (at_a - at_b)
        return ((at_x * CORES + from_core) * side + at_y) * cap + lax.rem(index, cap)

    def swap(zs):
        return pltpu.make_async_remote_copy(
            plane(own, zs), plane(peer, zs), swap_send.at[zs], swap_recv.at[zs],
            device_id=peer_device, device_id_type=MESH,
        )

    steps = [plane_of(t) for t in range(nz)]

    def against(ref, from_core, first, last):
        key = file_order(iota((plane_rows, 1), 0), from_core)
        query = file_order(iota((1, plane_rows), 1), core)
        limit = key < query
        for s in range(first, last + 1):
            zs = steps[s]
            fold(plane(ref, zs), plane(own, zs), zs, limit)
            for zt in steps[:s]:
                low, high = jnp.minimum(zs, zt), jnp.maximum(zs, zt)
                fold(plane(ref, low), plane(own, high), high, None)

    def work(what, first, last):
        @pl.when(is_owner)
        def _():
            if what == "meet":
                for zs in steps[first:last + 1]:
                    wait_for(plane(own, zs), plane_recv.at[zs])
                    swap(zs).start()
            elif what == "own":
                against(own, core, first, last)
            else:
                for zs in steps[first:last + 1]:
                    wait_for(plane(peer, zs), swap_recv.at[zs])
                against(peer, 1 - core, first, last)

    ready = [before(i)[0] + 1 if h > 1 else min(1, d // 3) for i, (d, h, _, _) in enumerate(order)]
    begins = [max(0, i + 1 - AHEAD, r) for i, r in enumerate(ready)]
    for i in range(1, len(begins)):
        begins[i] = max(begins[i], begins[i - 1])
    waited = set()
    sent_first = [i for i in range(2) if order[i][0] == 1]

    def line_ready(offset):
        if offset not in waited:
            waited.add(offset)
            wait_for(lined.at[z_at[offset]], line_recv.at[z_at[offset]])

    def send_after(count, direction):
        for index, (d, h, _, _) in enumerate(order):
            if begins[index] == count and index not in sent_first:
                if h == 1 and d > 1:
                    line_ready(d if direction == 0 else nz - d)
                pass_on(direction, index)

    pl.semaphore_wait(barrier, len(partners))
    for offset in (1, nz - 1):
        pack(z_at[offset])
        for index in sent_first:
            pass_on(0 if offset == 1 else 1, index)
    for offset in [sign * d % nz for d in range(2, far) for sign in (1, -1)] + [far, 0]:
        pack(z_at[offset])
        line_up(z_at[offset])
    for direction in range(2):
        send_after(0, direction)
    best[...] = jnp.full(best.shape, -float(width), F32)
    for count, message in enumerate(order, 1):
        d, h, _, _ = message
        for direction in range(2):
            buffer = held_by(direction, count - 1)
            wait_for(buffer, ring_recv.at[direction, count - 1])
            send_after(count, direction)
            if h == d:
                zs = z_at[nz - d if direction == 0 else d]
                first = first_of(direction, message)
                (spread_near if d == 1 else spread)(buffer, first, zs)
        if count == min(SPREAD_HERE, len(order)):
            line_ready(0)
            spread(lined.at[z], 0, z)
        for after, what, first, last in OWNER_WORK[far]:
            if after == count:
                work(what, first, last)
    @pl.when(is_owner)
    def _():
        result = jnp.max(best[...], axis=1, keepdims=True)
        result = jnp.maximum(result / width, -1.0)
        for piece in range(pieces):
            reply[:, piece] = result[:, :, piece * LANES:(piece + 1) * LANES]
        landing = home.at[(z * side + a) * per_line + lax.div(b, 2)]
        for oz in sorted(range(nz), key=lambda o: -min(o, nz - o)):
            for oa in range(side):
                for ob in range(side):
                    if (oz, oa, ob) == (0, 0, 0):
                        continue
                    target = b_at[ob] * side + a_at[oa]
                    pltpu.make_async_remote_copy(
                        reply.at[z_at[oz], lax.div(target, group)], landing,
                        reply_send, home_recv,
                        device_id=device(z_at[oz], a_at[oa], b_at[ob]), device_id_type=MESH,
                    ).start()
        pltpu.make_async_copy(reply.at[z, lax.div(place, group)], landing, home_recv).start()

    lane = lax.rem(place, group) * cap + rank
    wanted = jnp.concatenate([named.astype(BF16)] * 3, axis=0)
    answered = home.at[pl.ds(0, owners)]
    wait_for(answered, home_recv)
    left = answered[...].reshape(owners, LANES)
    split = []
    for _ in range(3):
        split.append(left.astype(BF16))
        left = left - split[-1].astype(F32)
    picked = lax.dot_general(
        jnp.concatenate(split, axis=0), wanted, (((0,), (0,)), ((), ())),
        preferred_element_type=F32,
    )
    out_ref[...] = jnp.sum(
        jnp.where(iota((LANES, rows), 0) == lane, picked, 0.0), axis=0, keepdims=True
    )

    lines = send.at[pl.ds(0, (nz - 2) * (side - 1))]
    wait_for(lines, line_send)
    for direction in range(2):
        parts = sum(message[3] for message in order) // per_line
        wait_for(ring.at[direction, pl.ds(0, parts)], ring_send)

    @pl.when(is_owner)
    def _():
        passed = 2 * (side * per_line - 1) + (nz - 2) * side * (per_line - 1)
        wait_for(own.at[pl.ds(0, passed)], plane_send)
        wait_for(home.at[pl.ds(0, nz * places - 1)], reply_send)
        for zs in range(nz):
            wait_for(plane(own, zs), swap_send.at[zs])

    @pl.when(jnp.logical_not(is_owner))
    def _():
        wait_for(own.at[pl.ds(0, nz * side * per_line)], plane_send)


def on_device(nz, side, cap, embed, cluster):
    rows, width = embed.shape
    places = side * side
    per_line = side // 2
    messages = len(RING_ORDER[nz // 2])
    pieces = places * cap // LANES
    out = pl.pallas_call(
        functools.partial(kernel, nz, side, cap),
        out_shape=jax.ShapeDtypeStruct((1, rows), F32),
        in_specs=[pl.BlockSpec(memory_space=pltpu.HBM)] * 2,
        out_specs=pl.BlockSpec(memory_space=pltpu.VMEM),
        scratch_shapes=[
            pltpu.VMEM((1, rows), jnp.int32),
            pltpu.VMEM((rows, width), BF16),
            pltpu.VMEM((rows, width), BF16),
            pltpu.VMEM((nz * side, per_line, cap, width), BF16),
            pltpu.VMEM((nz, side, per_line, cap, width), BF16),
            pltpu.VMEM((2, messages, per_line, per_line, cap, width), BF16),
            pltpu.VMEM((nz * places, cap, width), BF16),
            pltpu.VMEM((nz * places, cap, width), BF16),
            pltpu.VMEM((nz, 8, places * cap), F32),
            pltpu.VMEM((nz, pieces, 1, LANES), F32),
            pltpu.VMEM((nz * places, 1, LANES), F32),
            pltpu.SemaphoreType.DMA((2,)),
            pltpu.SemaphoreType.DMA,
            pltpu.SemaphoreType.DMA((nz,)),
            pltpu.SemaphoreType.DMA,
            pltpu.SemaphoreType.DMA((2, messages)),
            pltpu.SemaphoreType.DMA,
            pltpu.SemaphoreType.DMA((nz,)),
            pltpu.SemaphoreType.DMA((nz,)),
            pltpu.SemaphoreType.DMA((nz,)),
            pltpu.SemaphoreType.DMA,
            pltpu.SemaphoreType.DMA,
        ],
        compiler_params=pltpu.CompilerParams(
            collective_id=0, has_side_effects=True, vmem_limit_bytes=40 * 1024 * 1024
        ),
    )(
        pltpu.with_memory_space_constraint(cluster.reshape(1, rows), pltpu.HBM),
        pltpu.with_memory_space_constraint(embed, pltpu.HBM),
    )
    return out.reshape(rows)


def solution(mesh, cap=CAP):
    side = mesh.shape["grp"]
    nz = mesh.shape["shard"] // (CORES * side)
    return jax.shard_map(
        functools.partial(on_device, nz, side, cap),
        mesh=mesh,
        in_specs=(P(("shard", "grp"), None), P(("shard", "grp"), None)),
        out_specs=P(("shard", "grp")),
        check_vma=False,
    )
```

```python
import functools

import jax
import jax.numpy as jnp
from jax import lax
from jax.experimental import pallas as pl
from jax.experimental.pallas import tpu as pltpu
from jax.sharding import PartitionSpec as P

EPSILON = 1e-06
CORES = 2
CAP = 16
LANES = 128
MARK = 64.0
LOW = -1e30
MESH = pl.DeviceIdType.MESH
F32 = jnp.float32
BF16 = jnp.bfloat16


def iota(shape, dim):
    return lax.broadcasted_iota(jnp.int32, shape, dim)


def wait_for(ref, semaphore):
    pltpu.make_async_copy(ref, ref, semaphore).wait()


RING_ORDER = {
    2: ((2, 1, 0, 1), (1, 1, 0, 1), (2, 2, 0, 1), (1, 1, 1, 1)),
    4: (
        (1, 1, 0, 2), (1, 1, 2, 2), (2, 1, 0, 2), (2, 1, 2, 2), (3, 1, 0, 2), (2, 2, 0, 2),
        (2, 2, 2, 2), (3, 1, 2, 2), (3, 2, 0, 2), (4, 1, 0, 1), (4, 1, 1, 1), (3, 2, 2, 2),
        (3, 3, 0, 2), (4, 2, 0, 1), (4, 2, 1, 1), (3, 3, 2, 1), (4, 3, 0, 1), (4, 3, 1, 1),
        (3, 3, 3, 1), (4, 4, 0, 1), (4, 4, 1, 1),
    ),
}
AHEAD = 4
SPREAD_HERE = 5
OWNER_WORK = {
    2: (
        (4, "meet", 0, 2), (4, "own", 0, 2), (4, "peer", 0, 2),
        (4, "meet", 3, 3), (4, "own", 3, 3), (4, "peer", 3, 3),
    ),
    4: (
        (6, "meet", 0, 2), (7, "own", 0, 2), (8, "peer", 0, 2),
        (9, "meet", 3, 4), (9, "own", 3, 4), (11, "peer", 3, 4),
        (21, "meet", 5, 6), (21, "own", 5, 6), (21, "peer", 5, 5), (21, "meet", 7, 7),
        (21, "peer", 6, 6), (21, "own", 7, 7), (21, "peer", 7, 7),
    ),
}


def kernel(
    nz, side, cap,
    cluster_ref, embed_ref, out_ref,
    cluster_rows, embed, unit, send, lined, ring, own, peer, best, reply, home,
    fetch_sem, line_send, line_recv, ring_send, ring_recv, plane_send, plane_recv,
    swap_send, swap_recv, reply_send, home_recv,
):
    rows, width = embed.shape
    far = nz // 2
    places = side * side
    per_line = side // 2
    owners = nz * side * per_line
    block = side * per_line * cap
    plane_rows = places * cap
    pieces = plane_rows // LANES
    group = LANES // cap
    order = RING_ORDER[far]

    shard, y = lax.axis_index("shard"), lax.axis_index("grp")
    core = lax.rem(shard, CORES)
    x = lax.rem(lax.div(shard, CORES), side)
    z = lax.div(shard, CORES * side)
    a, b = x + core * (y - x), y + core * (x - y)
    place = b * side + a
    is_owner = lax.rem(x + y + z, 2) == 0
    z_at = [lax.rem(z + o, nz) for o in range(nz)]
    a_at = [lax.rem(a + o, side) for o in range(side)]
    b_at = [lax.rem(b + o, side) for o in range(side)]

    def device(zd, ad, bd):
        xd, yd = ad + core * (bd - ad), bd + core * (ad - bd)
        return ((zd * side + xd) * CORES + core, yd)

    peer_device = (shard + 1 - 2 * core, y)
    others = [(oa, ob) for oa in range(side) for ob in range(side) if (oa, ob) != (0, 0)]

    fetch_cluster = pltpu.make_async_copy(cluster_ref, cluster_rows, fetch_sem.at[0])
    fetch_embed = pltpu.make_async_copy(embed_ref, embed, fetch_sem.at[1])
    fetch_cluster.start()
    fetch_embed.start()

    barrier = pltpu.get_barrier_semaphore()
    partners = [device(z_at[o], a, b) for o in (1, nz - 1)]
    partners += [device(z, a_at[oa], b_at[ob]) for oa, ob in others]
    partners += [peer_device]
    for partner in partners:
        pl.semaphore_signal(barrier, inc=1, device_id=partner, device_id_type=MESH)

    fetch_cluster.wait()
    cluster = cluster_rows[...]
    to_z = lax.div(cluster, side * per_line)
    to_x = lax.rem(lax.div(cluster, per_line), side)
    to_y = 2 * lax.rem(cluster, per_line) + lax.rem(to_x + to_z, 2)
    to_a, to_b = to_x + core * (to_y - to_x), to_y + core * (to_x - to_y)
    owner = (to_z * side + to_a) * per_line + lax.div(to_b, 2)
    named = jnp.where(iota((owners, rows), 0) == owner, 1.0, 0.0)
    earlier = jnp.where(iota((rows, rows), 0) < iota((rows, rows), 1), 1.0, 0.0).astype(BF16)
    before = jnp.dot(named.astype(BF16), earlier, preferred_element_type=F32)
    rank = jnp.sum(before * named, axis=0, keepdims=True).astype(jnp.int32)
    slot = owner * cap + rank

    fetch_embed.wait()
    values = embed[...].astype(F32)
    mean_sq = jnp.sum(values * values, axis=1, keepdims=True) / width
    unit[...] = (values * lax.rsqrt(mean_sq + EPSILON)).astype(BF16)

    def pack(zo):
        chosen = jnp.where(iota((block, rows), 0) + zo * block == slot, 1.0, 0.0)
        packed = jnp.dot(chosen.astype(BF16), unit[...], preferred_element_type=F32)
        filled = jnp.sum(chosen, axis=1, keepdims=True)
        packed = jnp.where(filled > 0.5, packed, MARK).astype(BF16)
        send[pl.ds(zo * side, side)] = packed.reshape(side, per_line, cap, width)

    def line_up(zo):
        for o in range(1, side):
            pltpu.make_async_remote_copy(
                send.at[zo * side + a_at[o]], lined.at[zo, a], line_send, line_recv.at[zo],
                device_id=device(z, a_at[o], b), device_id_type=MESH,
            ).start()
        pltpu.make_async_copy(
            send.at[zo * side + a], lined.at[zo, a], line_recv.at[zo]
        ).start()

    def first_of(direction, message):
        return message[2] + (direction * per_line if message[0] == far else 0)

    def held_by(direction, index):
        return ring.at[direction, index, pl.ds(0, order[index][3])]

    def before(index):
        d, h, first, count = order[index]
        for i, (e, hop, start, held) in enumerate(order):
            if (e, hop) == (d, h - 1) and start <= first and first + count <= start + held:
                return i, first - start
        return -1, 0

    def pass_on(direction, index):
        d, h, _, count = order[index]
        if h > 1:
            source, start = before(index)
            source = ring.at[direction, source, pl.ds(start, count)]
        else:
            zo = z_at[d if direction == 0 else nz - d]
            first = first_of(direction, order[index])
            if d == 1:
                source = send.at[pl.ds(zo * side + first, count)]
            else:
                source = lined.at[zo, pl.ds(first, count)]
        pltpu.make_async_remote_copy(
            source, held_by(direction, index), ring_send, ring_recv.at[direction, index],
            device_id=device(z_at[1 if direction == 0 else nz - 1], a, b), device_id_type=MESH,
        ).start()

    def spread(source, first, zs):
        landing = own.at[pl.ds((zs * side + b) * side + first, source.shape[0])]
        for g in range(per_line):
            owner_b = 2 * g + lax.rem(a + z, 2)
            part = source.at[:, g]

            @pl.when(b == owner_b)
            def _():
                pltpu.make_async_copy(part, landing, plane_recv.at[zs]).start()

            @pl.when(b != owner_b)
            def _():
                pltpu.make_async_remote_copy(
                    part, landing, plane_send, plane_recv.at[zs],
                    device_id=device(z, a, owner_b), device_id_type=MESH,
                ).start()

    def spread_near(source, first, zs):
        landing = own.at[(zs * side + b) * side + a]
        for i in range(per_line):
            for g in range(per_line):
                owner_a = first + i
                owner_b = 2 * g + lax.rem(owner_a + z, 2)
                mine = (a == owner_a) & (b == owner_b)

                @pl.when(mine)
                def _():
                    pltpu.make_async_copy(source.at[i, g], landing, plane_recv.at[zs]).start()

                @pl.when(jnp.logical_not(mine))
                def _():
                    pltpu.make_async_remote_copy(
                        source.at[i, g], landing, plane_send, plane_recv.at[zs],
                        device_id=device(z, owner_a, owner_b), device_id_type=MESH,
                    ).start()

    def plane(ref, index):
        return ref.at[pl.ds(index * places, places)]

    def fold(keys, queries, query_plane, limit):
        found = keys[...].reshape(plane_rows, width)
        asked = queries[...].reshape(plane_rows, width)
        scores = lax.dot_general(
            found, asked, (((1,), (1,)), ((), ())), preferred_element_type=F32
        )
        bias = jnp.where(found[:, :LANES].astype(F32) > 32.0, LOW, 0.0)
        scores = scores + jnp.concatenate([bias] * pieces, axis=1)
        if limit is not None:
            scores = jnp.where(limit, scores, LOW)
        top = jnp.max(scores.reshape(plane_rows // 8, 8, plane_rows), axis=0)
        best[query_plane] = jnp.maximum(best[query_plane], top)

    def plane_of(t):
        return z_at[(2 * (t % 2) - 1) * ((t + 1) // 2) % nz]

    def file_order(index, from_core):
        at_b, at_a = lax.div(index, side * cap), lax.rem(lax.div(index, cap), side)
        at_x, at_y = at_a + from_core * (at_b - at_a), at_b + from_core * (at_a - at_b)
        return ((at_x * CORES + from_core) * side + at_y) * cap + lax.rem(index, cap)

    def swap(zs):
        return pltpu.make_async_remote_copy(
            plane(own, zs), plane(peer, zs), swap_send.at[zs], swap_recv.at[zs],
            device_id=peer_device, device_id_type=MESH,
        )

    steps = [plane_of(t) for t in range(nz)]

    def against(ref, from_core, first, last):
        key = file_order(iota((plane_rows, 1), 0), from_core)
        query = file_order(iota((1, plane_rows), 1), core)
        limit = key < query
        for s in range(first, last + 1):
            zs = steps[s]
            fold(plane(ref, zs), plane(own, zs), zs, limit)
            for zt in steps[:s]:
                low, high = jnp.minimum(zs, zt), jnp.maximum(zs, zt)
                fold(plane(ref, low), plane(own, high), high, None)

    def work(what, first, last):
        @pl.when(is_owner)
        def _():
            if what == "meet":
                for zs in steps[first:last + 1]:
                    wait_for(plane(own, zs), plane_recv.at[zs])
                    swap(zs).start()
            elif what == "own":
                against(own, core, first, last)
            else:
                for zs in steps[first:last + 1]:
                    wait_for(plane(peer, zs), swap_recv.at[zs])
                against(peer, 1 - core, first, last)

    ready = [before(i)[0] + 1 if h > 1 else min(1, d // 3) for i, (d, h, _, _) in enumerate(order)]
    begins = [max(0, i + 1 - AHEAD, r) for i, r in enumerate(ready)]
    if far > 2:
        begins[3] = 1
    for i in range(1, len(begins)):
        begins[i] = max(begins[i], begins[i - 1])
    waited = set()
    sent_first = [i for i in range(2) if order[i][0] == 1]

    def line_ready(offset):
        if offset not in waited:
            waited.add(offset)
            wait_for(lined.at[z_at[offset]], line_recv.at[z_at[offset]])

    def send_after(count, direction):
        for index, (d, h, _, _) in enumerate(order):
            if begins[index] == count and index not in sent_first:
                if h == 1 and d > 1:
                    line_ready(d if direction == 0 else nz - d)
                pass_on(direction, index)

    pl.semaphore_wait(barrier, len(partners))
    for offset in (1, nz - 1):
        pack(z_at[offset])
        for index in sent_first:
            pass_on(0 if offset == 1 else 1, index)
    for offset in [sign * d % nz for d in range(2, far) for sign in (1, -1)] + [far, 0]:
        pack(z_at[offset])
        line_up(z_at[offset])
    for direction in range(2):
        send_after(0, direction)
    best[...] = jnp.full(best.shape, -float(width), F32)
    for count, message in enumerate(order, 1):
        d, h, _, _ = message
        for direction in range(2):
            buffer = held_by(direction, count - 1)
            wait_for(buffer, ring_recv.at[direction, count - 1])
            send_after(count, direction)
            if h == d:
                zs = z_at[nz - d if direction == 0 else d]
                first = first_of(direction, message)
                (spread_near if d == 1 else spread)(buffer, first, zs)
        if count == min(SPREAD_HERE, len(order)):
            line_ready(0)
            spread(lined.at[z], 0, z)
        for after, what, first, last in OWNER_WORK[far]:
            if after == count:
                work(what, first, last)
    @pl.when(is_owner)
    def _():
        result = jnp.max(best[...], axis=1, keepdims=True)
        result = jnp.maximum(result / width, -1.0)
        for piece in range(pieces):
            reply[:, piece] = result[:, :, piece * LANES:(piece + 1) * LANES]
        landing = home.at[(z * side + a) * per_line + lax.div(b, 2)]
        for oz in sorted(range(nz), key=lambda o: -min(o, nz - o)):
            for oa in range(side):
                for ob in range(side):
                    if (oz, oa, ob) == (0, 0, 0):
                        continue
                    target = b_at[ob] * side + a_at[oa]
                    pltpu.make_async_remote_copy(
                        reply.at[z_at[oz], lax.div(target, group)], landing,
                        reply_send, home_recv,
                        device_id=device(z_at[oz], a_at[oa], b_at[ob]), device_id_type=MESH,
                    ).start()
        pltpu.make_async_copy(reply.at[z, lax.div(place, group)], landing, home_recv).start()

    lane = lax.rem(place, group) * cap + rank
    wanted = jnp.concatenate([named.astype(BF16)] * 3, axis=0)
    answered = home.at[pl.ds(0, owners)]
    wait_for(answered, home_recv)
    left = answered[...].reshape(owners, LANES)
    split = []
    for _ in range(3):
        split.append(left.astype(BF16))
        left = left - split[-1].astype(F32)
    picked = lax.dot_general(
        jnp.concatenate(split, axis=0), wanted, (((0,), (0,)), ((), ())),
        preferred_element_type=F32,
    )
    out_ref[...] = jnp.sum(
        jnp.where(iota((LANES, rows), 0) == lane, picked, 0.0), axis=0, keepdims=True
    )

    lines = send.at[pl.ds(0, (nz - 2) * (side - 1))]
    wait_for(lines, line_send)
    for direction in range(2):
        parts = sum(message[3] for message in order) // per_line
        wait_for(ring.at[direction, pl.ds(0, parts)], ring_send)

    @pl.when(is_owner)
    def _():
        passed = 2 * (side * per_line - 1) + (nz - 2) * side * (per_line - 1)
        wait_for(own.at[pl.ds(0, passed)], plane_send)
        wait_for(home.at[pl.ds(0, nz * places - 1)], reply_send)
        for zs in range(nz):
            wait_for(plane(own, zs), swap_send.at[zs])

    @pl.when(jnp.logical_not(is_owner))
    def _():
        wait_for(own.at[pl.ds(0, nz * side * per_line)], plane_send)


def on_device(nz, side, cap, embed, cluster):
    rows, width = embed.shape
    places = side * side
    per_line = side // 2
    messages = len(RING_ORDER[nz // 2])
    pieces = places * cap // LANES
    out = pl.pallas_call(
        functools.partial(kernel, nz, side, cap),
        out_shape=jax.ShapeDtypeStruct((1, rows), F32),
        in_specs=[pl.BlockSpec(memory_space=pltpu.HBM)] * 2,
        out_specs=pl.BlockSpec(memory_space=pltpu.VMEM),
        scratch_shapes=[
            pltpu.VMEM((1, rows), jnp.int32),
            pltpu.VMEM((rows, width), BF16),
            pltpu.VMEM((rows, width), BF16),
            pltpu.VMEM((nz * side, per_line, cap, width), BF16),
            pltpu.VMEM((nz, side, per_line, cap, width), BF16),
            pltpu.VMEM((2, messages, per_line, per_line, cap, width), BF16),
            pltpu.VMEM((nz * places, cap, width), BF16),
            pltpu.VMEM((nz * places, cap, width), BF16),
            pltpu.VMEM((nz, 8, places * cap), F32),
            pltpu.VMEM((nz, pieces, 1, LANES), F32),
            pltpu.VMEM((nz * places, 1, LANES), F32),
            pltpu.SemaphoreType.DMA((2,)),
            pltpu.SemaphoreType.DMA,
            pltpu.SemaphoreType.DMA((nz,)),
            pltpu.SemaphoreType.DMA,
            pltpu.SemaphoreType.DMA((2, messages)),
            pltpu.SemaphoreType.DMA,
            pltpu.SemaphoreType.DMA((nz,)),
            pltpu.SemaphoreType.DMA((nz,)),
            pltpu.SemaphoreType.DMA((nz,)),
            pltpu.SemaphoreType.DMA,
            pltpu.SemaphoreType.DMA,
        ],
        compiler_params=pltpu.CompilerParams(
            collective_id=0, has_side_effects=True, vmem_limit_bytes=40 * 1024 * 1024
        ),
    )(
        pltpu.with_memory_space_constraint(cluster.reshape(1, rows), pltpu.HBM),
        pltpu.with_memory_space_constraint(embed, pltpu.HBM),
    )
    return out.reshape(rows)


def solution(mesh, cap=CAP):
    side = mesh.shape["grp"]
    nz = mesh.shape["shard"] // (CORES * side)
    return jax.shard_map(
        functools.partial(on_device, nz, side, cap),
        mesh=mesh,
        in_specs=(P(("shard", "grp"), None), P(("shard", "grp"), None)),
        out_specs=P(("shard", "grp")),
        check_vma=False,
    )
```

```python
import functools

import jax
import jax.numpy as jnp
from jax import lax
from jax.experimental import pallas as pl
from jax.experimental.pallas import tpu as pltpu
from jax.sharding import PartitionSpec as P

EPSILON = 1e-06
CORES = 2
CAP = 16
LANES = 128
MARK = 64.0
LOW = -1e30
MESH = pl.DeviceIdType.MESH
F32 = jnp.float32
BF16 = jnp.bfloat16


def iota(shape, dim):
    return lax.broadcasted_iota(jnp.int32, shape, dim)


def wait_for(ref, semaphore):
    pltpu.make_async_copy(ref, ref, semaphore).wait()


RING_ORDER = {
    2: ((2, 1, 0, 1), (1, 1, 0, 1), (2, 2, 0, 1), (1, 1, 1, 1)),
    4: (
        (1, 1, 0, 2), (1, 1, 2, 2), (2, 1, 0, 2), (2, 1, 2, 2), (3, 1, 0, 2), (2, 2, 0, 2),
        (2, 2, 2, 2), (3, 1, 2, 2), (3, 2, 0, 2), (4, 1, 0, 1), (4, 1, 1, 1), (3, 2, 2, 2),
        (3, 3, 0, 2), (4, 2, 0, 1), (4, 2, 1, 1), (3, 3, 2, 1), (4, 3, 0, 1), (4, 3, 1, 1),
        (3, 3, 3, 1), (4, 4, 0, 1), (4, 4, 1, 1),
    ),
}
AHEAD = 4
SPREAD_HERE = 5
OWNER_WORK = {
    2: (
        (4, "meet", 0, 2), (4, "own", 0, 2), (4, "peer", 0, 2),
        (4, "meet", 3, 3), (4, "own", 3, 3), (4, "peer", 3, 3),
    ),
    4: (
        (6, "meet", 0, 2), (7, "own", 0, 2), (8, "peer", 0, 2),
        (9, "meet", 3, 4), (9, "own", 3, 4), (11, "peer", 3, 4),
        (21, "meet", 5, 6), (21, "own", 5, 6), (21, "meet", 7, 7), (21, "own", 7, 7),
        (21, "peer", 5, 6), (21, "peer", 7, 7),
    ),
}


def kernel(
    nz, side, cap,
    cluster_ref, embed_ref, out_ref,
    cluster_rows, embed, unit, send, lined, ring, own, peer, best, reply, home,
    fetch_sem, line_send, line_recv, ring_send, ring_recv, plane_send, plane_recv,
    swap_send, swap_recv, reply_send, home_recv,
):
    rows, width = embed.shape
    far = nz // 2
    places = side * side
    per_line = side // 2
    owners = nz * side * per_line
    block = side * per_line * cap
    plane_rows = places * cap
    pieces = plane_rows // LANES
    group = LANES // cap
    order = RING_ORDER[far]

    shard, y = lax.axis_index("shard"), lax.axis_index("grp")
    core = lax.rem(shard, CORES)
    x = lax.rem(lax.div(shard, CORES), side)
    z = lax.div(shard, CORES * side)
    a, b = x + core * (y - x), y + core * (x - y)
    place = b * side + a
    is_owner = lax.rem(x + y + z, 2) == 0
    z_at = [lax.rem(z + o, nz) for o in range(nz)]
    a_at = [lax.rem(a + o, side) for o in range(side)]
    b_at = [lax.rem(b + o, side) for o in range(side)]

    def device(zd, ad, bd):
        xd, yd = ad + core * (bd - ad), bd + core * (ad - bd)
        return ((zd * side + xd) * CORES + core, yd)

    peer_device = (shard + 1 - 2 * core, y)
    others = [(oa, ob) for oa in range(side) for ob in range(side) if (oa, ob) != (0, 0)]

    fetch_cluster = pltpu.make_async_copy(cluster_ref, cluster_rows, fetch_sem.at[0])
    fetch_embed = pltpu.make_async_copy(embed_ref, embed, fetch_sem.at[1])
    fetch_cluster.start()
    fetch_embed.start()

    barrier = pltpu.get_barrier_semaphore()
    partners = [device(z_at[o], a, b) for o in (1, nz - 1)]
    partners += [device(z, a_at[oa], b_at[ob]) for oa, ob in others]
    partners += [peer_device]
    for partner in partners:
        pl.semaphore_signal(barrier, inc=1, device_id=partner, device_id_type=MESH)

    fetch_cluster.wait()
    cluster = cluster_rows[...]
    to_z = lax.div(cluster, side * per_line)
    to_x = lax.rem(lax.div(cluster, per_line), side)
    to_y = 2 * lax.rem(cluster, per_line) + lax.rem(to_x + to_z, 2)
    to_a, to_b = to_x + core * (to_y - to_x), to_y + core * (to_x - to_y)
    owner = (to_z * side + to_a) * per_line + lax.div(to_b, 2)
    named = jnp.where(iota((owners, rows), 0) == owner, 1.0, 0.0)
    earlier = jnp.where(iota((rows, rows), 0) < iota((rows, rows), 1), 1.0, 0.0).astype(BF16)
    before = jnp.dot(named.astype(BF16), earlier, preferred_element_type=F32)
    rank = jnp.sum(before * named, axis=0, keepdims=True).astype(jnp.int32)
    slot = owner * cap + rank

    fetch_embed.wait()
    values = embed[...].astype(F32)
    mean_sq = jnp.sum(values * values, axis=1, keepdims=True) / width
    unit[...] = (values * lax.rsqrt(mean_sq + EPSILON)).astype(BF16)

    def pack(zo):
        chosen = jnp.where(iota((block, rows), 0) + zo * block == slot, 1.0, 0.0)
        packed = jnp.dot(chosen.astype(BF16), unit[...], preferred_element_type=F32)
        filled = jnp.sum(chosen, axis=1, keepdims=True)
        packed = jnp.where(filled > 0.5, packed, MARK).astype(BF16)
        send[pl.ds(zo * side, side)] = packed.reshape(side, per_line, cap, width)

    def line_up(zo):
        for o in range(1, side):
            pltpu.make_async_remote_copy(
                send.at[zo * side + a_at[o]], lined.at[zo, a], line_send, line_recv.at[zo],
                device_id=device(z, a_at[o], b), device_id_type=MESH,
            ).start()
        pltpu.make_async_copy(
            send.at[zo * side + a], lined.at[zo, a], line_recv.at[zo]
        ).start()

    def first_of(direction, message):
        return message[2] + (direction * per_line if message[0] == far else 0)

    def held_by(direction, index):
        return ring.at[direction, index, pl.ds(0, order[index][3])]

    def before(index):
        d, h, first, count = order[index]
        for i, (e, hop, start, held) in enumerate(order):
            if (e, hop) == (d, h - 1) and start <= first and first + count <= start + held:
                return i, first - start
        return -1, 0

    def pass_on(direction, index):
        d, h, _, count = order[index]
        if h > 1:
            source, start = before(index)
            source = ring.at[direction, source, pl.ds(start, count)]
        else:
            zo = z_at[d if direction == 0 else nz - d]
            first = first_of(direction, order[index])
            if d == 1:
                source = send.at[pl.ds(zo * side + first, count)]
            else:
                source = lined.at[zo, pl.ds(first, count)]
        pltpu.make_async_remote_copy(
            source, held_by(direction, index), ring_send, ring_recv.at[direction, index],
            device_id=device(z_at[1 if direction == 0 else nz - 1], a, b), device_id_type=MESH,
        ).start()

    def spread(source, first, zs):
        landing = own.at[pl.ds((zs * side + b) * side + first, source.shape[0])]
        for g in range(per_line):
            owner_b = 2 * g + lax.rem(a + z, 2)
            part = source.at[:, g]

            @pl.when(b == owner_b)
            def _():
                pltpu.make_async_copy(part, landing, plane_recv.at[zs]).start()

            @pl.when(b != owner_b)
            def _():
                pltpu.make_async_remote_copy(
                    part, landing, plane_send, plane_recv.at[zs],
                    device_id=device(z, a, owner_b), device_id_type=MESH,
                ).start()

    def spread_near(source, first, zs):
        landing = own.at[(zs * side + b) * side + a]
        for i in range(per_line):
            for g in range(per_line):
                owner_a = first + i
                owner_b = 2 * g + lax.rem(owner_a + z, 2)
                mine = (a == owner_a) & (b == owner_b)

                @pl.when(mine)
                def _():
                    pltpu.make_async_copy(source.at[i, g], landing, plane_recv.at[zs]).start()

                @pl.when(jnp.logical_not(mine))
                def _():
                    pltpu.make_async_remote_copy(
                        source.at[i, g], landing, plane_send, plane_recv.at[zs],
                        device_id=device(z, owner_a, owner_b), device_id_type=MESH,
                    ).start()

    def plane(ref, index):
        return ref.at[pl.ds(index * places, places)]

    def fold(keys, queries, query_plane, limit):
        found = keys[...].reshape(plane_rows, width)
        asked = queries[...].reshape(plane_rows, width)
        scores = lax.dot_general(
            found, asked, (((1,), (1,)), ((), ())), preferred_element_type=F32
        )
        bias = jnp.where(found[:, :LANES].astype(F32) > 32.0, LOW, 0.0)
        scores = scores + jnp.concatenate([bias] * pieces, axis=1)
        if limit is not None:
            scores = jnp.where(limit, scores, LOW)
        top = jnp.max(scores.reshape(plane_rows // 8, 8, plane_rows), axis=0)
        best[query_plane] = jnp.maximum(best[query_plane], top)

    def plane_of(t):
        return z_at[(2 * (t % 2) - 1) * ((t + 1) // 2) % nz]

    def file_order(index, from_core):
        at_b, at_a = lax.div(index, side * cap), lax.rem(lax.div(index, cap), side)
        at_x, at_y = at_a + from_core * (at_b - at_a), at_b + from_core * (at_a - at_b)
        return ((at_x * CORES + from_core) * side + at_y) * cap + lax.rem(index, cap)

    def swap(zs):
        return pltpu.make_async_remote_copy(
            plane(own, zs), plane(peer, zs), swap_send.at[zs], swap_recv.at[zs],
            device_id=peer_device, device_id_type=MESH,
        )

    steps = [plane_of(t) for t in range(nz)]

    def against(ref, from_core, first, last):
        key = file_order(iota((plane_rows, 1), 0), from_core)
        query = file_order(iota((1, plane_rows), 1), core)
        limit = key < query
        for s in range(first, last + 1):
            zs = steps[s]
            fold(plane(ref, zs), plane(own, zs), zs, limit)
            for zt in steps[:s]:
                low, high = jnp.minimum(zs, zt), jnp.maximum(zs, zt)
                fold(plane(ref, low), plane(own, high), high, None)

    def work(what, first, last):
        @pl.when(is_owner)
        def _():
            if what == "meet":
                for zs in steps[first:last + 1]:
                    wait_for(plane(own, zs), plane_recv.at[zs])
                    swap(zs).start()
            elif what == "own":
                against(own, core, first, last)
            else:
                for zs in steps[first:last + 1]:
                    wait_for(plane(peer, zs), swap_recv.at[zs])
                against(peer, 1 - core, first, last)

    ready = [before(i)[0] + 1 if h > 1 else min(1, d // 3) for i, (d, h, _, _) in enumerate(order)]
    begins = [max(0, i + 1 - AHEAD, r) for i, r in enumerate(ready)]
    if far > 2:
        begins[3] = 1
    for i in range(1, len(begins)):
        begins[i] = max(begins[i], begins[i - 1])
    waited = set()
    sent_first = [i for i in range(2) if order[i][0] == 1]

    def line_ready(offset):
        if offset not in waited:
            waited.add(offset)
            wait_for(lined.at[z_at[offset]], line_recv.at[z_at[offset]])

    def send_after(count, direction):
        for index, (d, h, _, _) in enumerate(order):
            if begins[index] == count and index not in sent_first:
                if h == 1 and d > 1:
                    line_ready(d if direction == 0 else nz - d)
                pass_on(direction, index)

    pl.semaphore_wait(barrier, len(partners))
    for offset in (1, nz - 1):
        pack(z_at[offset])
        for index in sent_first:
            pass_on(0 if offset == 1 else 1, index)
    for offset in [sign * d % nz for d in range(2, far) for sign in (1, -1)] + [far, 0]:
        pack(z_at[offset])
        line_up(z_at[offset])
    for direction in range(2):
        send_after(0, direction)
    best[...] = jnp.full(best.shape, -float(width), F32)
    for count, message in enumerate(order, 1):
        d, h, _, _ = message
        for direction in range(2):
            buffer = held_by(direction, count - 1)
            wait_for(buffer, ring_recv.at[direction, count - 1])
            send_after(count, direction)
            if h == d:
                zs = z_at[nz - d if direction == 0 else d]
                first = first_of(direction, message)
                (spread_near if d == 1 else spread)(buffer, first, zs)
        if count == min(SPREAD_HERE, len(order)):
            line_ready(0)
            spread(lined.at[z], 0, z)
        for after, what, first, last in OWNER_WORK[far]:
            if after == count:
                work(what, first, last)
    @pl.when(is_owner)
    def _():
        result = jnp.max(best[...], axis=1, keepdims=True)
        result = jnp.maximum(result / width, -1.0)
        for piece in range(pieces):
            reply[:, piece] = result[:, :, piece * LANES:(piece + 1) * LANES]
        landing = home.at[(z * side + a) * per_line + lax.div(b, 2)]
        for oz in sorted(range(nz), key=lambda o: -min(o, nz - o)):
            for oa in range(side):
                for ob in range(side):
                    if (oz, oa, ob) == (0, 0, 0):
                        continue
                    target = b_at[ob] * side + a_at[oa]
                    pltpu.make_async_remote_copy(
                        reply.at[z_at[oz], lax.div(target, group)], landing,
                        reply_send, home_recv,
                        device_id=device(z_at[oz], a_at[oa], b_at[ob]), device_id_type=MESH,
                    ).start()
        pltpu.make_async_copy(reply.at[z, lax.div(place, group)], landing, home_recv).start()

    lane = lax.rem(place, group) * cap + rank
    wanted = jnp.concatenate([named.astype(BF16)] * 3, axis=0)
    answered = home.at[pl.ds(0, owners)]
    wait_for(answered, home_recv)
    left = answered[...].reshape(owners, LANES)
    split = []
    for _ in range(3):
        split.append(left.astype(BF16))
        left = left - split[-1].astype(F32)
    picked = lax.dot_general(
        jnp.concatenate(split, axis=0), wanted, (((0,), (0,)), ((), ())),
        preferred_element_type=F32,
    )
    out_ref[...] = jnp.sum(
        jnp.where(iota((LANES, rows), 0) == lane, picked, 0.0), axis=0, keepdims=True
    )

    lines = send.at[pl.ds(0, (nz - 2) * (side - 1))]
    wait_for(lines, line_send)
    for direction in range(2):
        parts = sum(message[3] for message in order) // per_line
        wait_for(ring.at[direction, pl.ds(0, parts)], ring_send)

    @pl.when(is_owner)
    def _():
        passed = 2 * (side * per_line - 1) + (nz - 2) * side * (per_line - 1)
        wait_for(own.at[pl.ds(0, passed)], plane_send)
        wait_for(home.at[pl.ds(0, nz * places - 1)], reply_send)
        for zs in range(nz):
            wait_for(plane(own, zs), swap_send.at[zs])

    @pl.when(jnp.logical_not(is_owner))
    def _():
        wait_for(own.at[pl.ds(0, nz * side * per_line)], plane_send)


def on_device(nz, side, cap, embed, cluster):
    rows, width = embed.shape
    places = side * side
    per_line = side // 2
    messages = len(RING_ORDER[nz // 2])
    pieces = places * cap // LANES
    out = pl.pallas_call(
        functools.partial(kernel, nz, side, cap),
        out_shape=jax.ShapeDtypeStruct((1, rows), F32),
        in_specs=[pl.BlockSpec(memory_space=pltpu.HBM)] * 2,
        out_specs=pl.BlockSpec(memory_space=pltpu.VMEM),
        scratch_shapes=[
            pltpu.VMEM((1, rows), jnp.int32),
            pltpu.VMEM((rows, width), BF16),
            pltpu.VMEM((rows, width), BF16),
            pltpu.VMEM((nz * side, per_line, cap, width), BF16),
            pltpu.VMEM((nz, side, per_line, cap, width), BF16),
            pltpu.VMEM((2, messages, per_line, per_line, cap, width), BF16),
            pltpu.VMEM((nz * places, cap, width), BF16),
            pltpu.VMEM((nz * places, cap, width), BF16),
            pltpu.VMEM((nz, 8, places * cap), F32),
            pltpu.VMEM((nz, pieces, 1, LANES), F32),
            pltpu.VMEM((nz * places, 1, LANES), F32),
            pltpu.SemaphoreType.DMA((2,)),
            pltpu.SemaphoreType.DMA,
            pltpu.SemaphoreType.DMA((nz,)),
            pltpu.SemaphoreType.DMA,
            pltpu.SemaphoreType.DMA((2, messages)),
            pltpu.SemaphoreType.DMA,
            pltpu.SemaphoreType.DMA((nz,)),
            pltpu.SemaphoreType.DMA((nz,)),
            pltpu.SemaphoreType.DMA((nz,)),
            pltpu.SemaphoreType.DMA,
            pltpu.SemaphoreType.DMA,
        ],
        compiler_params=pltpu.CompilerParams(
            collective_id=0, has_side_effects=True, vmem_limit_bytes=40 * 1024 * 1024
        ),
    )(
        pltpu.with_memory_space_constraint(cluster.reshape(1, rows), pltpu.HBM),
        pltpu.with_memory_space_constraint(embed, pltpu.HBM),
    )
    return out.reshape(rows)


def solution(mesh, cap=CAP):
    side = mesh.shape["grp"]
    nz = mesh.shape["shard"] // (CORES * side)
    return jax.shard_map(
        functools.partial(on_device, nz, side, cap),
        mesh=mesh,
        in_specs=(P(("shard", "grp"), None), P(("shard", "grp"), None)),
        out_specs=P(("shard", "grp")),
        check_vma=False,
    )
```
